128 devices in a mesh: slide: 4 (over x), seq: 32 (over z, y, core).
Axes of the slice: x: 4, y: 4, z: 4, core: 2. Of those that a mesh axis runs over, the one named last changes fastest.
Arguments:
- tiles: bfloat16 [32768, 1536], P(('slide', 'seq')), may hold values from -6 to 6
- dest_row: int32 [32768], replicated, may hold values from 0 to 32767, as said below
- w_in: bfloat16 [1536, 768], replicated, may hold values from -0.15625 to 0.15625
- norm_gain: float32 [768], replicated, may hold values from 0.25 to 1.75
- w_query: bfloat16 [768, 768], replicated
- w_key: bfloat16 [768, 768], replicated
- w_value: bfloat16 [768, 768], replicated, may hold values from -0.21875 to 0.21875
- w_out: bfloat16 [768, 768], replicated, may hold values from -0.21875 to 0.21875
- out_grad: bfloat16 [32768, 768], P(('slide', 'seq')), may hold values from -6 to 6
Outputs:
- layer_out: bfloat16 [32768, 768], P(('slide', 'seq'))
- tile_grads: bfloat16 [32768, 1536], P(('slide', 'seq'))
The draws below stay inside these ranges and needn't reach their ends.
Inputs may be any that keep to these rules, and one draw needn't show every extreme that they name: `dest_row`: A permutation of the rows of the slide-major sequence. The 256 tiles of one device go to at most 4 rows of the block of 256 rows held by any one device, and some pairs of devices reach 4 in every draw.
All inputs are finite; a program needn't handle non-finite values.
Results may differ from the reference program's by a relative error of at most 0.015.
Values may be sent and summed in bfloat16 or wider, within the bound.
A program may use at most 128 MiB of HBM per device.

```python
import jax
import jax.numpy as jnp
import numpy as np
from jax import lax

TILE_W = 1536
HEADS = 12
HEAD_DIM = 64
STRIDE = 16
TILE_DEV = 256
D = 768
SENDERS = 128
TILES = 32768
KEYS = 512
N_SLIDE = 4
N_SEQ = 32


def shared_matrix(key):
    return jax.random.normal(key, (D, D), jnp.float32) * D ** (-0.5)


def draw_w_query(key, part):
    common = shared_matrix(key)
    return common.astype(jnp.bfloat16)


def draw_w_key(key, part):
    key = jax.random.fold_in(key, 9)
    first_key = jax.random.fold_in(key, 0)
    fresh = jax.random.normal(first_key, (D, D), jnp.float32) * D ** (-0.5)
    return fresh.astype(jnp.bfloat16)


def draw_dest_row(key, part):
    key = jax.random.fold_in(key, 11)
    first_key, second_key, third_key = jax.random.split(key, 3)
    count = SENDERS
    share = TILE_DEV // count
    first = jax.random.permutation(first_key, count).astype(jnp.int32)
    offset = jax.random.randint(second_key, (), 1, count).astype(jnp.int32)
    second = first[(jnp.arange(count, dtype=jnp.int32) + offset) % count]
    columns = jnp.arange(count, dtype=jnp.int32)
    counts = share + share * (columns[None, :] == first[:, None]).astype(jnp.int32) - share * (columns[None, :] == second[:, None]).astype(jnp.int32)
    before = jnp.cumsum(counts, axis=0) - counts
    upto = jnp.cumsum(counts, axis=1)
    slots = jnp.arange(TILE_DEV, dtype=jnp.int32)
    target = jnp.sum((upto[:, None, :] <= slots[None, :, None]).astype(jnp.int32), axis=2)
    lower = jnp.take_along_axis(upto - counts, target, axis=1)
    start = jnp.take_along_axis(before, target, axis=1)
    dest = target * TILE_DEV + start + slots[None, :] - lower
    orders = jax.vmap(lambda k: jax.random.permutation(k, TILE_DEV))(jax.random.split(third_key, count)).astype(jnp.int32)
    sources = jnp.broadcast_to(jnp.arange(count, dtype=jnp.int32)[:, None], (count, TILE_DEV))
    placed = jnp.zeros((count, TILE_DEV), jnp.int32).at[sources, orders].set(dest)
    return placed.reshape(TILES)


def block_levels(stream_key, dims, cuts, least, high):
    level, own = 1.0, jax.random.fold_in(stream_key, 6)
    for position, blocks in cuts:
        draws = jnp.exp(jax.random.uniform(jax.random.fold_in(own, position), (blocks,), jnp.float32, least / len(cuts), high / len(cuts)))
        level = level * jnp.repeat(draws, dims[position] // blocks).reshape([-1 if axis == position else 1 for axis in range(len(dims))])
    return level


def centred(stream_key, dims, scale, reach, cuts=(), kind=jnp.bfloat16):
    entries = scale * jax.random.normal(stream_key, dims, jnp.float32)
    if cuts:
        entries = entries * block_levels(stream_key, dims, cuts, -0.22, 0.18)
    return jnp.clip(entries, -reach, reach).astype(kind)


def setup_inputs(seed: int = 0) -> dict:
    arg_keys = jax.random.split(jax.random.key(seed), 10)
    tiles = centred(arg_keys[0], (TILES, TILE_W), 1.0, 6.0, ((0, 128),))
    dest_row = draw_dest_row(jax.random.fold_in(arg_keys[9], 71), 0)
    w_in = centred(arg_keys[2], (TILE_W, D), TILE_W ** -0.5, 0.15625)
    norm_gain = jnp.clip(1.0 + 0.15 * jax.random.normal(arg_keys[3], (D,), jnp.float32), 0.25, 1.75)
    w_query = draw_w_query(jax.random.fold_in(arg_keys[9], 71), 0)
    w_key = draw_w_key(jax.random.fold_in(arg_keys[9], 71), 0)
    w_value = centred(arg_keys[6], (D, D), D ** -0.5, 0.21875)
    w_out = centred(arg_keys[7], (D, D), D ** -0.5, 0.21875)
    out_grad = centred(arg_keys[8], (TILES, D), 1.0, 6.0, ((0, 128),))
    return dict(tiles=tiles, dest_row=dest_row, w_in=w_in, norm_gain=norm_gain, w_query=w_query, w_key=w_key, w_value=w_value, w_out=w_out, out_grad=out_grad)


def project(data, weight):
    return jnp.dot(data, weight, preferred_element_type=jnp.float32).astype(jnp.bfloat16)

def backproject(data, weight):
    return lax.dot_general(data, weight, (((1,), (1,)), ((), ())), preferred_element_type=jnp.float32)

def normalize(hidden):
    values = hidden.astype(jnp.float32)
    centre = lax.optimization_barrier(jnp.mean(values, axis=1, keepdims=True))
    centered = values - centre
    spread = lax.optimization_barrier(jnp.mean(centered * centered, axis=1, keepdims=True))
    inverse = lax.rsqrt(spread + 1e-05)
    return (centered * inverse, inverse)

def norm_backward(grad_normed, normalized, inverse, gain, out_grad):
    scaled = grad_normed * gain
    inner = scaled - lax.optimization_barrier(jnp.mean(scaled, axis=1, keepdims=True)) - normalized * lax.optimization_barrier(jnp.mean(scaled * normalized, axis=1, keepdims=True))
    return (out_grad.astype(jnp.float32) + inner * inverse).astype(jnp.bfloat16)

def split_heads(matrix, heads):
    return matrix.reshape(matrix.shape[0], heads, -1).transpose(1, 0, 2)

def merge_heads(matrix):
    return matrix.transpose(1, 0, 2).reshape(matrix.shape[1], -1)

def select_dilated(matrix, heads, stride):
    count, width = matrix.shape
    grid = matrix.reshape(count // stride, stride, heads, width // heads)
    picks = grid[:, np.arange(heads) % stride, np.arange(heads), :]
    return picks.reshape(count // stride, width)

def place_dilated(matrix, part, heads, stride):
    count, width = matrix.shape
    grid = matrix.reshape(count // stride, stride, heads, width // heads)
    grid = grid.at[:, np.arange(heads) % stride, np.arange(heads), :].add(part.reshape(count // stride, heads, width // heads))
    return grid.reshape(count, width)

def contract_rows(left, right):
    return lax.dot_general(left, right, (((1,), (1,)), ((), ())), preferred_element_type=jnp.float32)

def contract_cols(left, right):
    return lax.dot_general(left, right, (((0,), (0,)), ((), ())), preferred_element_type=jnp.float32)

def head_probs(query, near_key, far_key):
    scale = 1.0 / np.sqrt(query.shape[-1])
    near = contract_rows(query, near_key) * scale
    far = contract_rows(query, far_key) * scale
    top = jnp.maximum(lax.optimization_barrier(jnp.max(near, axis=1, keepdims=True)), lax.optimization_barrier(jnp.max(far, axis=1, keepdims=True)))
    near_exp = jnp.exp(near - top)
    far_exp = jnp.exp(far - top)
    total = lax.optimization_barrier(jnp.sum(near_exp, axis=1, keepdims=True)) + lax.optimization_barrier(jnp.sum(far_exp, axis=1, keepdims=True))
    return (near_exp / total, far_exp / total)

def head_forward(parts):
    query, near_key, near_value, far_key, far_value = parts
    near_p, far_p = head_probs(query, near_key, far_key)
    mixed = jnp.dot(near_p.astype(jnp.bfloat16), near_value, preferred_element_type=jnp.float32)
    mixed = mixed + jnp.dot(far_p.astype(jnp.bfloat16), far_value, preferred_element_type=jnp.float32)
    return mixed.astype(jnp.bfloat16)

def head_backward(parts):
    query, near_key, near_value, far_key, far_value, upstream = parts
    scale = 1.0 / np.sqrt(query.shape[-1])
    near_p, far_p = head_probs(query, near_key, far_key)
    near_w = near_p.astype(jnp.bfloat16)
    far_w = far_p.astype(jnp.bfloat16)
    near_dp = contract_rows(upstream, near_value)
    far_dp = contract_rows(upstream, far_value)
    delta = lax.optimization_barrier(jnp.sum(near_p * near_dp, axis=1, keepdims=True)) + lax.optimization_barrier(jnp.sum(far_p * far_dp, axis=1, keepdims=True))
    near_ds = (near_p * (near_dp - delta) * scale).astype(jnp.bfloat16)
    far_ds = (far_p * (far_dp - delta) * scale).astype(jnp.bfloat16)
    d_query = jnp.dot(near_ds, near_key, preferred_element_type=jnp.float32) + jnp.dot(far_ds, far_key, preferred_element_type=jnp.float32)
    return (d_query, contract_cols(near_ds, query), contract_cols(near_w, upstream), contract_cols(far_ds, query), contract_cols(far_w, upstream))

def attend_forward(query, near_key, near_value, far_key, far_value, heads):
    stacked = tuple((split_heads(m, heads) for m in (query, near_key, near_value, far_key, far_value)))
    return merge_heads(lax.map(head_forward, stacked))

def attend_backward(query, near_key, near_value, far_key, far_value, upstream, heads):
    stacked = tuple((split_heads(m, heads) for m in (query, near_key, near_value, far_key, far_value, upstream)))
    return tuple((merge_heads(m) for m in lax.map(head_backward, stacked)))

def reference(tiles, dest_row, w_in, norm_gain, w_query, w_key, w_value, w_out, out_grad):
    blocks = N_SLIDE * N_SEQ
    width = HEADS * HEAD_DIM
    sequence_tiles = jnp.zeros_like(tiles).at[dest_row].set(tiles)
    hidden = project(sequence_tiles, w_in)
    normalized, inverse = normalize(hidden)
    normed = (normalized * norm_gain).astype(jnp.bfloat16)
    query = project(normed, w_query).reshape(blocks, TILE_DEV, width)
    key = project(normed, w_key).reshape(blocks, TILE_DEV, width)
    value = project(normed, w_value).reshape(blocks, TILE_DEV, width)
    far_key = jax.vmap(lambda m: select_dilated(m, HEADS, STRIDE))(key).reshape(N_SLIDE, KEYS, width)
    far_value = jax.vmap(lambda m: select_dilated(m, HEADS, STRIDE))(value).reshape(N_SLIDE, KEYS, width)
    slide_of = (jnp.arange(blocks) // N_SEQ).astype(jnp.int32)

    def block_forward(parts):
        q_block, k_block, v_block, slide = parts
        return attend_forward(q_block, k_block, v_block, far_key[slide], far_value[slide], HEADS)
    attended = lax.map(block_forward, (query, key, value, slide_of)).reshape(TILES, width)
    layer_out = (hidden.astype(jnp.float32) + jnp.dot(attended, w_out, preferred_element_type=jnp.float32)).astype(jnp.bfloat16)
    grad_attended = backproject(out_grad, w_out).astype(jnp.bfloat16).reshape(blocks, TILE_DEV, width)

    def block_backward(parts):
        q_block, k_block, v_block, g_block, slide = parts
        return attend_backward(q_block, k_block, v_block, far_key[slide], far_value[slide], g_block, HEADS)
    d_query, d_key, d_value, d_far_key, d_far_value = lax.map(block_backward, (query, key, value, grad_attended, slide_of))
    rows_back = TILE_DEV // STRIDE
    back_key = d_far_key.reshape(N_SLIDE, N_SEQ, KEYS, width).sum(axis=1).reshape(blocks, rows_back, width)
    back_value = d_far_value.reshape(N_SLIDE, N_SEQ, KEYS, width).sum(axis=1).reshape(blocks, rows_back, width)
    d_key = jax.vmap(lambda m, p: place_dilated(m, p, HEADS, STRIDE))(d_key, back_key)
    d_value = jax.vmap(lambda m, p: place_dilated(m, p, HEADS, STRIDE))(d_value, back_value)
    grad_query = d_query.reshape(TILES, width).astype(jnp.bfloat16)
    grad_key = d_key.reshape(TILES, width).astype(jnp.bfloat16)
    grad_value = d_value.reshape(TILES, width).astype(jnp.bfloat16)
    grad_normed = backproject(grad_query, w_query) + backproject(grad_key, w_key) + backproject(grad_value, w_value)
    grad_hidden = norm_backward(grad_normed, normalized, inverse, norm_gain, out_grad)
    grad_sequence = backproject(grad_hidden, w_in).astype(jnp.bfloat16)
    tile_grads = grad_sequence[dest_row]
    return (layer_out, tile_grads)
```

```python
import functools

import jax
import jax.numpy as jnp
from jax import lax
from jax.experimental import pallas as pl
from jax.experimental.pallas import tpu as pltpu
from jax.sharding import PartitionSpec as P

ROWS = 256
WIDTH = 1536
D = 768
DEVICES = 128
SLOTS = 4
PACKED = DEVICES * SLOTS
CHIPS = 16
FAR = 16
HALF = CHIPS * FAR
PAIRS = 6
LANES = 128
MESH = pl.DeviceIdType.MESH
F32 = jnp.float32
BF16 = jnp.bfloat16
VMEM_LIMIT = 56 * 1024 * 1024


def mm(left, right):
    return jnp.dot(left, right, preferred_element_type=F32)


def mm_nt(left, right):
    return lax.dot_general(left, right, (((1,), (1,)), ((), ())), preferred_element_type=F32)


def iota(shape, dim):
    return lax.broadcasted_iota(jnp.int32, shape, dim)


def onehot(cond):
    return jnp.where(cond, 1.0, 0.0).astype(BF16)


def my_index():
    return lax.axis_index("slide") * 32 + lax.axis_index("seq")


def send_targets(dest_ref):
    own = dest_ref[pl.ds(my_index(), 1), :]
    target = jnp.broadcast_to((own // ROWS).astype(F32), (ROWS, ROWS))
    across = target.T
    same = across == target
    earlier_row = jnp.where(same & (iota((ROWS, ROWS), 0) < iota((ROWS, ROWS), 1)), 1.0, 0.0)
    earlier_col = jnp.where(same & (iota((ROWS, ROWS), 1) < iota((ROWS, ROWS), 0)), 1.0, 0.0)
    slot_row = target[0:1, :] * SLOTS + jnp.sum(earlier_row, axis=0, keepdims=True)
    slot_col = across[:, 0:1] * SLOTS + jnp.sum(earlier_col, axis=1, keepdims=True)
    return slot_row.astype(jnp.int32), slot_col.astype(jnp.int32)


def receive_positions(dest_ref):
    dest = dest_ref[...].astype(F32).T.astype(jnp.int32)
    mine = dest // ROWS == my_index()
    before = onehot(iota((ROWS, ROWS), 1) < iota((ROWS, ROWS), 0))
    rank = mm(before, onehot(mine))
    place = jnp.where(mine, (dest % ROWS).astype(F32) + 1.0, 0.0)
    total = jnp.zeros((8, PACKED), F32)
    for k in range(SLOTS):
        held = jnp.sum(jnp.where(rank == k, place, 0.0), axis=0, keepdims=True)
        spread = onehot(iota((DEVICES, PACKED), 1) == iota((DEVICES, PACKED), 0) * SLOTS + k)
        total = total + mm(jnp.broadcast_to(held, (8, DEVICES)).astype(BF16), spread)
    return total - 1.0


def rows_to_slots(rows_ref, slots_ref):
    def step(i, carry):
        two = rows_ref[pl.ds(pl.multiple_of(i * 8, 8), 8), :].astype(BF16)
        slots_ref[2 * i] = two[0:4]
        slots_ref[2 * i + 1] = two[4:8]
        return carry

    lax.fori_loop(0, DEVICES // 2, step, 0, unroll=8)


def slots_to_rows(slots_ref, rows_ref):
    def step(i, carry):
        first = slots_ref[2 * i].astype(F32)
        second = slots_ref[2 * i + 1].astype(F32)
        rows_ref[pl.ds(pl.multiple_of(i * 8, 8), 8), :] = jnp.concatenate([first, second], axis=0)
        return carry

    lax.fori_loop(0, DEVICES // 2, step, 0, unroll=8)


def send_kernel(tiles_ref, dest_ref, w_in_ref, packed_ref, rows_ref):
    hidden = mm(tiles_ref[...], w_in_ref[...]).astype(BF16)
    slot_row, _ = send_targets(dest_ref)
    pack = onehot(iota((PACKED, ROWS), 0) == slot_row)
    rows_ref[...] = mm(pack, hidden)
    rows_to_slots(rows_ref, packed_ref)


def return_kernel(arrived_ref, dest_ref, w_in_ref, grads_ref, rows_ref):
    slots_to_rows(arrived_ref, rows_ref)
    _, slot_col = send_targets(dest_ref)
    pick = onehot(iota((ROWS, PACKED), 1) == slot_col)
    grad_hidden = mm(pick, rows_ref[...].astype(BF16)).astype(BF16)
    grads_ref[...] = mm_nt(grad_hidden, w_in_ref[...]).astype(BF16)


def head_of_row():
    return iota((ROWS, D), 0) % 16 == iota((ROWS, D), 1) // 64


def normalize(hidden):
    centre = jnp.mean(hidden, axis=1, keepdims=True)
    centered = hidden - centre
    spread = jnp.mean(centered * centered, axis=1, keepdims=True)
    inverse = lax.rsqrt(spread + 1e-05)
    return centered * inverse, inverse


def block_kernel(
    arrived_ref, dest_ref, gain_ref, wq_ref, wk_ref, wv_ref, wo_ref, og_ref,
    layer_ref, packed_ref,
    rows_ref, hidden_ref, q_ref, k_ref, v_ref, g_ref, far_ref,
    att_ref, dq_ref, dk_ref, dv_ref,
    keep_ref, half_send, half_recv, part_send, part_recv,
    g_send, g_recv, f_send, f_recv, h_send, h_recv, p_send, p_recv,
):
    slide = lax.axis_index("slide")
    seq = lax.axis_index("seq")
    chip, core = seq // 2, seq % 2
    z, y = chip // 4, chip % 4
    partner = (slide, seq + 1 - 2 * core)

    def ahead(r):
        return ((z + r // 4) % 4) * 4 + (y + r % 4) % 4

    def behind(r):
        return ((z + 4 - r // 4) % 4) * 4 + (y + 4 - r % 4) % 4

    def same_core(other):
        return (slide, other * 2 + core)

    def chip_rows(other):
        return pl.ds(pl.multiple_of(other * FAR, FAR), FAR)

    def partner_rows(other):
        return pl.ds(pl.multiple_of(HALF + other * FAR, FAR), FAR)

    barrier = pltpu.get_barrier_semaphore()

    def greet(r, carry):
        pl.semaphore_signal(barrier, inc=1, device_id=same_core(ahead(r)), device_id_type=MESH)
        return carry

    lax.fori_loop(1, CHIPS, greet, 0)
    pl.semaphore_signal(barrier, inc=1, device_id=partner, device_id_type=MESH)

    slots_to_rows(arrived_ref, rows_ref)
    position = receive_positions(dest_ref)
    place = onehot(iota((ROWS, PACKED), 0).astype(F32) == position[0:1, :])
    hidden = mm(place, rows_ref[...].astype(BF16))
    hidden_ref[...] = hidden.astype(BF16)
    normalized, _ = normalize(hidden)
    normed = (normalized * gain_ref[...]).astype(BF16)
    k_ref[...] = mm(normed, wk_ref[...]).astype(BF16)
    v_ref[...] = mm(normed, wv_ref[...]).astype(BF16)

    chosen = head_of_row()
    pick = onehot(iota((FAR, ROWS), 0) == iota((FAR, ROWS), 1) // 16)
    none = jnp.zeros((ROWS, D), BF16)
    own = chip_rows(chip)
    far_ref[own, 0:D] = mm(pick, jnp.where(chosen, k_ref[...], none)).astype(BF16)
    far_ref[own, D:] = mm(pick, jnp.where(chosen, v_ref[...], none)).astype(BF16)

    pl.semaphore_wait(barrier, CHIPS)

    def gather_copy(r):
        return pltpu.make_async_remote_copy(
            src_ref=far_ref.at[own], dst_ref=far_ref.at[own],
            send_sem=g_send.at[r], recv_sem=g_recv.at[r],
            device_id=same_core(ahead(r)), device_id_type=MESH,
        )

    def forward_copy(r):
        source = behind(r)
        return pltpu.make_async_remote_copy(
            src_ref=far_ref.at[chip_rows(source)], dst_ref=far_ref.at[partner_rows(source)],
            send_sem=f_send.at[r], recv_sem=f_recv.at[r],
            device_id=partner, device_id_type=MESH,
        )

    def send_own(r, carry):
        gather_copy(r).start()
        return carry

    forward_copy(0).start()
    lax.fori_loop(1, CHIPS, send_own, 0)

    q_ref[...] = mm(normed, wq_ref[...]).astype(BF16) * jnp.bfloat16(0.125)
    g_ref[...] = mm_nt(og_ref[...], wo_ref[...]).astype(BF16)

    def pass_on(r, carry):
        gather_copy(r).wait_recv()
        forward_copy(r).start()
        return carry

    lax.fori_loop(1, CHIPS, pass_on, 0)

    def arrive(r, carry):
        forward_copy(r).wait_recv()
        return carry

    lax.fori_loop(0, CHIPS, arrive, 0)

    def half_copy(c):
        return pltpu.make_async_remote_copy(
            src_ref=half_send.at[c], dst_ref=half_recv.at[c],
            send_sem=h_send.at[c], recv_sem=h_recv.at[c],
            device_id=partner, device_id_type=MESH,
        )

    def share(c):
        half_copy(c).wait_recv()
        part_send[c] = (keep_ref[c] + half_recv[c].astype(F32)).astype(BF16)
        part_recv[c, own] = part_send[c, own]

        def send_part(r, carry):
            other = ahead(r)
            pltpu.make_async_remote_copy(
                src_ref=part_send.at[c, chip_rows(other)], dst_ref=part_recv.at[c, own],
                send_sem=p_send.at[c, r], recv_sem=p_recv.at[c, r],
                device_id=same_core(other), device_id_type=MESH,
            ).start()
            return carry

        lax.fori_loop(1, CHIPS, send_part, 0)

    low = iota((ROWS, LANES), 1) < 64
    zero = jnp.zeros((ROWS, LANES), BF16)

    def both(pair):
        return jnp.concatenate([jnp.where(low, pair, zero), jnp.where(low, zero, pair)], axis=0)

    def mixed(near_t, far_t, near_w, far_w):
        first = mm(near_t[:64], near_w[:, :ROWS]) + mm(far_t[:64], far_w[:, :ROWS])
        second = mm(near_t[64:], near_w[:, ROWS:]) + mm(far_t[64:], far_w[:, ROWS:])
        return jnp.concatenate([first, second], axis=0).T

    def attend(c, carry):
        cols = pl.ds(pl.multiple_of(c * LANES, LANES), LANES)
        value_cols = pl.ds(pl.multiple_of(D + c * LANES, LANES), LANES)
        q2, g2 = both(q_ref[:, cols]), both(g_ref[:, cols])
        kn, vn = k_ref[:, cols], v_ref[:, cols]
        kf, vf = far_ref[:, cols], far_ref[:, value_cols]
        sn, sf = mm_nt(kn, q2), mm_nt(kf, q2)
        top = jnp.maximum(jnp.max(sn, axis=0, keepdims=True), jnp.max(sf, axis=0, keepdims=True))
        en, ef = jnp.exp(sn - top), jnp.exp(sf - top)
        inv = 1.0 / (jnp.sum(en, axis=0, keepdims=True) + jnp.sum(ef, axis=0, keepdims=True))
        pn, pf = en * inv, ef * inv
        wn, wf = pn.astype(BF16), pf.astype(BF16)
        dn, df = mm_nt(vn, g2), mm_nt(vf, g2)
        delta = jnp.sum(pn * dn, axis=0, keepdims=True) + jnp.sum(pf * df, axis=0, keepdims=True)
        tn, tf = (pn * (dn - delta)).astype(BF16), (pf * (df - delta)).astype(BF16)
        dkf, dvf = mm(tf, q2), mm(wf, g2)
        keep_ref[c, :, :LANES] = dkf[:HALF]
        keep_ref[c, :, LANES:] = dvf[:HALF]
        half_send[c, :, :LANES] = dkf[HALF:].astype(BF16)
        half_send[c, :, LANES:] = dvf[HALF:].astype(BF16)
        half_copy(c).start()
        dk_ref[:, cols] = mm(tn, q2)
        dv_ref[:, cols] = mm(wn, g2)
        att_ref[:, cols] = mixed(vn.T, vf.T, wn, wf).astype(BF16)
        dq_ref[:, cols] = (mixed(kn.T, kf.T, tn, tf) * 0.125).astype(BF16)

        @pl.when(c > 0)
        def _():
            share(c - 1)

        return carry

    lax.fori_loop(0, PAIRS, attend, 0)
    share(PAIRS - 1)

    hidden = hidden_ref[...].astype(F32)
    layer_ref[...] = (hidden + mm(att_ref[...], wo_ref[...])).astype(BF16)
    grad_normed = mm_nt(dq_ref[...], wq_ref[...])

    def part_wait(c, carry):
        def one(r, inner):
            other = ahead(r)
            pltpu.make_async_remote_copy(
                src_ref=part_send.at[c, chip_rows(other)], dst_ref=part_recv.at[c, chip_rows(behind(r))],
                send_sem=p_send.at[c, r], recv_sem=p_recv.at[c, r],
                device_id=same_core(other), device_id_type=MESH,
            ).wait()
            return inner

        lax.fori_loop(1, CHIPS, one, 0)
        half_copy(c).wait_send()
        cols = pl.ds(pl.multiple_of(c * LANES, LANES), LANES)
        total = jnp.sum(part_recv[c].astype(F32).reshape(CHIPS, FAR, 2 * LANES), axis=0)
        spread = jnp.broadcast_to(total[:, None, :], (FAR, 16, 2 * LANES)).reshape(ROWS, 2 * LANES)
        seen = iota((ROWS, LANES), 0) % 16 == iota((ROWS, LANES), 1) // 64 + 2 * c
        dk_ref[:, cols] += jnp.where(seen, spread[:, :LANES], 0.0)
        dv_ref[:, cols] += jnp.where(seen, spread[:, LANES:], 0.0)
        return carry

    lax.fori_loop(0, PAIRS, part_wait, 0)

    grad_normed = grad_normed + mm_nt(dk_ref[...].astype(BF16), wk_ref[...])
    grad_normed = grad_normed + mm_nt(dv_ref[...].astype(BF16), wv_ref[...])
    normalized, inverse = normalize(hidden)
    scaled = grad_normed * gain_ref[...]
    inner = (
        scaled
        - jnp.mean(scaled, axis=1, keepdims=True)
        - normalized * jnp.mean(scaled * normalized, axis=1, keepdims=True)
    )
    grad_hidden = (og_ref[...].astype(F32) + inner * inverse).astype(BF16)

    column = position.T[:, 0:1]
    unplace = onehot(iota((PACKED, ROWS), 1).astype(F32) == column)
    rows_ref[...] = mm(unplace, grad_hidden)
    rows_to_slots(rows_ref, packed_ref)

    def sent(r, carry):
        gather_copy(r).wait_send()
        return carry

    def passed(r, carry):
        forward_copy(r).wait_send()
        return carry

    lax.fori_loop(1, CHIPS, sent, 0)
    lax.fori_loop(0, CHIPS, passed, 0)


def exchange(packed):
    return lax.all_to_all(packed, ("slide", "seq"), split_axis=0, concat_axis=0, tiled=True)


def per_device(tiles, dest_row, w_in, norm_gain, w_query, w_key, w_value, w_out, out_grad):
    dest = dest_row.reshape(DEVICES, ROWS)
    vmem = pl.BlockSpec(memory_space=pltpu.VMEM)
    slots = jax.ShapeDtypeStruct((DEVICES, SLOTS, D), BF16)
    rows = pltpu.VMEM((PACKED, D), F32)
    params = pltpu.CompilerParams(vmem_limit_bytes=VMEM_LIMIT)
    packed = pl.pallas_call(
        send_kernel, out_shape=slots, in_specs=[vmem] * 3, out_specs=vmem,
        scratch_shapes=[rows], compiler_params=params,
    )(tiles, dest, w_in)
    arrived = exchange(packed)
    dma = pltpu.SemaphoreType.DMA
    layer_out, packed = pl.pallas_call(
        block_kernel,
        out_shape=(jax.ShapeDtypeStruct((ROWS, D), BF16), slots),
        in_specs=[vmem] * 8,
        out_specs=(vmem, vmem),
        scratch_shapes=[
            rows,
            pltpu.VMEM((ROWS, D), BF16),
            pltpu.VMEM((ROWS, D), BF16),
            pltpu.VMEM((ROWS, D), BF16),
            pltpu.VMEM((ROWS, D), BF16),
            pltpu.VMEM((ROWS, D), BF16),
            pltpu.VMEM((2 * HALF, 2 * D), BF16),
            pltpu.VMEM((ROWS, D), BF16),
            pltpu.VMEM((ROWS, D), BF16),
            pltpu.VMEM((ROWS, D), F32),
            pltpu.VMEM((ROWS, D), F32),
            pltpu.VMEM((PAIRS, HALF, 2 * LANES), F32),
            pltpu.VMEM((PAIRS, HALF, 2 * LANES), BF16),
            pltpu.VMEM((PAIRS, HALF, 2 * LANES), BF16),
            pltpu.VMEM((PAIRS, HALF, 2 * LANES), BF16),
            pltpu.VMEM((PAIRS, HALF, 2 * LANES), BF16),
            dma((CHIPS,)), dma((CHIPS,)), dma((CHIPS,)), dma((CHIPS,)),
            dma((PAIRS,)), dma((PAIRS,)), dma((PAIRS, CHIPS)), dma((PAIRS, CHIPS)),
        ],
        compiler_params=pltpu.CompilerParams(
            vmem_limit_bytes=VMEM_LIMIT, collective_id=0, has_side_effects=True
        ),
    )(arrived, dest, norm_gain.reshape(1, D), w_query, w_key, w_value, w_out, out_grad)
    arrived = exchange(packed)
    tile_grads = pl.pallas_call(
        return_kernel, out_shape=jax.ShapeDtypeStruct((ROWS, WIDTH), BF16), in_specs=[vmem] * 3,
        out_specs=vmem, scratch_shapes=[rows], compiler_params=params,
    )(arrived, dest, w_in)
    return layer_out, tile_grads


def solution(mesh):
    split = P(("slide", "seq"), None)
    return jax.shard_map(
        per_device,
        mesh=mesh,
        in_specs=(split, P(), P(), P(), P(), P(), P(), P(), split),
        out_specs=(split, split),
        check_vma=False,
    )
```

```python
import jax
import jax.numpy as jnp
from jax import lax
from jax.experimental import pallas as pl
from jax.experimental.pallas import tpu as pltpu
from jax.sharding import PartitionSpec as P

ROWS = 256
WIDTH = 1536
D = 768
DEVICES = 128
SLOTS = 4
PACKED = DEVICES * SLOTS
ALL_CHIPS = 64
GROUPS = 4
GROUP = ALL_CHIPS // GROUPS
MIX = 37
UNMIX = 45
CHIPS = 16
FAR = 16
HALF = CHIPS * FAR
PAIRS = 6
LANES = 128
MESH = pl.DeviceIdType.MESH
F32 = jnp.float32
BF16 = jnp.bfloat16
VMEM_LIMIT = 56 * 1024 * 1024


def mm(left, right):
    return jnp.dot(left, right, preferred_element_type=F32)


def mm_nt(left, right):
    return lax.dot_general(left, right, (((1,), (1,)), ((), ())), preferred_element_type=F32)


def iota(shape, dim):
    return lax.broadcasted_iota(jnp.int32, shape, dim)


def onehot(cond):
    return jnp.where(cond, 1.0, 0.0).astype(BF16)


def where_am_i():
    slide, seq = lax.axis_index("slide"), lax.axis_index("seq")
    return slide, seq // 8, (seq // 2) % 4, seq % 2


def message_of(device, sign):
    slide, z, y, core = where_am_i()
    by_slide = (sign * (device // 32 - slide)) & 3
    by_z = (sign * ((device // 8) % 4 - z)) & 3
    by_y = (sign * ((device // 2) % 4 - y)) & 3
    offset = by_slide * 16 + by_z * 4 + by_y
    return (offset * UNMIX) & 63, device % 2


def own_targets(dest_ref):
    slide, z, y, core = where_am_i()
    me = slide * 32 + z * 8 + y * 2 + core
    own = jnp.concatenate([dest_ref[pl.ds(2 * me, 1), :], dest_ref[pl.ds(2 * me + 1, 1), :]], axis=1)
    device = jnp.broadcast_to(own // ROWS, (ROWS, ROWS))
    target = device.astype(F32)
    across = target.T
    same = across == target
    before_row = iota((ROWS, ROWS), 0) < iota((ROWS, ROWS), 1)
    before_col = iota((ROWS, ROWS), 1) < iota((ROWS, ROWS), 0)
    rank_row = jnp.sum(jnp.where(same & before_row, 1.0, 0.0), axis=0, keepdims=True)
    rank_col = jnp.sum(jnp.where(same & before_col, 1.0, 0.0), axis=1, keepdims=True)
    row = message_of(device[0:1, :], 1)
    col = message_of(across[:, 0:1].astype(jnp.int32), 1)
    send_row = row[0] * 8 + row[1] * SLOTS + rank_row.astype(jnp.int32)
    back_col = (col[1] ^ core) * (PACKED // 2) + col[0] * SLOTS + rank_col.astype(jnp.int32)
    return send_row, back_col


def receive_positions(dest_ref):
    slide, z, y, core = where_am_i()
    me = slide * 32 + z * 8 + y * 2 + core
    half = ROWS // 2
    dest = dest_ref[...].astype(F32).T.astype(jnp.int32)
    mine = dest // ROWS == me
    marks = onehot(mine)
    before = onehot(iota((half, half), 1) < iota((half, half), 0))
    lane = iota((ROWS, ROWS), 1)
    first_half = onehot((iota((ROWS, ROWS), 0) == lane - 1) & (lane % 2 == 1))
    count = mm(jnp.ones((half, half), BF16), marks).astype(BF16)
    rank = mm(before, marks) + mm(count, first_half)
    place = jnp.where(mine, (dest % ROWS).astype(F32) + 1.0, 0.0)
    message, sender_core = message_of(iota((ROWS, 1), 0) // 2, -1)
    slot = (sender_core ^ core) * (PACKED // 2) + message * SLOTS
    column = iota((ROWS, PACKED), 1)
    total = jnp.zeros((8, PACKED), F32)
    for k in range(SLOTS):
        held = jnp.sum(jnp.where(rank == k, place, 0.0), axis=0, keepdims=True)
        total = total + mm(jnp.broadcast_to(held, (8, ROWS)).astype(BF16), onehot(column == slot + k))
    return total - 1.0


def head_of_row():
    return iota((ROWS, D), 0) % 16 == iota((ROWS, D), 1) // 64


def normalize(hidden):
    centre = jnp.mean(hidden, axis=1, keepdims=True)
    centered = hidden - centre
    spread = jnp.mean(centered * centered, axis=1, keepdims=True)
    inverse = lax.rsqrt(spread + 1e-05)
    return centered * inverse, inverse


def block_kernel(
    tiles_hbm, dest_ref, gain_ref, w_in_hbm, wq_hbm, wk_hbm, wv_hbm, wo_hbm, og_hbm,
    layer_ref, back_ref,
    tiles_ref, w_in_ref, wq_ref, wk_ref, wv_ref, wo_ref, og_ref,
    rows_ref, out_ref, mid_ref, over_ref, out2_ref, mid2_ref, over2_ref,
    hidden_ref, q_ref, k_ref, v_ref, g_ref, far_ref,
    att_ref, dq_ref, dk_ref, dv_ref,
    keep_ref, half_send, half_recv, part_send, part_recv,
    load_sem, x_send, x_recv, o_send, o_recv,
    g_send, g_recv, f_send, f_recv, h_send, h_recv, p_send, p_recv,
):
    slide, z, y, core = where_am_i()
    chip = z * 4 + y
    other_core = 1 - core
    partner = (slide, chip * 2 + other_core)

    def ahead(r):
        return ((z + r // 4) % 4) * 4 + (y + r % 4) % 4

    def same_core(other):
        return (slide, other * 2 + core)

    def chip_rows(other):
        return pl.ds(pl.multiple_of(other * FAR, FAR), FAR)

    def at_offset(offset):
        to_slide = (slide + offset // 16) % 4
        to_z = (z + (offset // 4) % 4) % 4
        to_y = (y + offset % 4) % 4
        return (to_slide, (to_z * 4 + to_y) * 2 + core)

    def loop(first, last, do):
        def step(i, carry):
            do(i)
            return carry

        lax.fori_loop(first, last, step, 0)

    loads = [
        pltpu.make_async_copy(source, target, load_sem.at[i])
        for i, (source, target) in enumerate(
            [
                (tiles_hbm, tiles_ref), (w_in_hbm, w_in_ref), (og_hbm, og_ref), (wo_hbm, wo_ref),
                (wk_hbm, wk_ref), (wv_hbm, wv_ref), (wq_hbm, wq_ref),
            ]
        )
    ]
    for load in loads:
        load.start()

    barrier = pltpu.get_barrier_semaphore()

    def greet(j):
        device = at_offset((j * MIX) & 63)
        pl.semaphore_signal(barrier, inc=1, device_id=device, device_id_type=MESH)

    loop(1, ALL_CHIPS, greet)
    pl.semaphore_signal(barrier, inc=1, device_id=partner, device_id_type=MESH)

    def message(way, j, source, landing):
        offset = (j * MIX) & 63
        device = at_offset(offset) if way == 0 else at_offset(
            ((4 - offset // 16) % 4) * 16 + ((4 - (offset // 4) % 4) % 4) * 4 + (4 - offset % 4) % 4
        )
        return pltpu.make_async_remote_copy(
            src_ref=source.at[j], dst_ref=landing.at[j],
            send_sem=x_send.at[way], recv_sem=x_recv.at[way, j // GROUP],
            device_id=device, device_id_type=MESH,
        )

    def hand_over(way, group, landing, over):
        part = pl.ds(group * GROUP, GROUP)
        return pltpu.make_async_remote_copy(
            src_ref=landing.at[part, other_core], dst_ref=over.at[part],
            send_sem=o_send.at[way, group], recv_sem=o_recv.at[way, group],
            device_id=partner, device_id_type=MESH,
        )

    def exchange_start(way, source, landing):
        loop(1, ALL_CHIPS, lambda j: message(way, j, source, landing).start())
        landing[0] = source[0]

    def exchange_arrive(way, source, landing, over):
        for group in range(GROUPS):
            arrived = pl.ds(group * GROUP + (group == 0), GROUP - (group == 0))
            pltpu.make_async_copy(source.at[arrived], landing.at[arrived], x_recv.at[way, group]).wait()
            hand_over(way, group, landing, over).start()

    def own_rows(landing):
        def step(i, carry):
            first = landing[2 * i, core].astype(F32)
            second = landing[2 * i + 1, core].astype(F32)
            rows_ref[pl.ds(pl.multiple_of(i * 8, 8), 8), :] = jnp.concatenate([first, second], axis=0)
            return carry

        lax.fori_loop(0, ALL_CHIPS // 2, step, 0, unroll=8)

    def over_rows(way, landing, over):
        for group in range(GROUPS):
            hand_over(way, group, landing, over).wait_recv()

        def step(i, carry):
            first = over[2 * i].astype(F32)
            second = over[2 * i + 1].astype(F32)
            start = pl.multiple_of(PACKED // 2 + i * 8, 8)
            rows_ref[pl.ds(start, 8), :] = jnp.concatenate([first, second], axis=0)
            return carry

        lax.fori_loop(0, ALL_CHIPS // 2, step, 0, unroll=8)

    def exchange_sent(way, source, landing, over):
        left = pl.ds(1, ALL_CHIPS - 1)
        pltpu.make_async_copy(source.at[left], landing.at[left], x_send.at[way]).wait()
        for group in range(GROUPS):
            hand_over(way, group, landing, over).wait_send()

    send_row, back_col = own_targets(dest_ref)
    pack = onehot(iota((PACKED, ROWS), 0) == send_row)
    pick_back = onehot(iota((ROWS, PACKED), 1) == back_col)
    loads[0].wait()
    loads[1].wait()
    rows_ref[...] = mm(pack, mm(tiles_ref[...], w_in_ref[...]).astype(BF16))

    def pack_step(j, carry):
        rows = rows_ref[pl.ds(pl.multiple_of(j * 8, 8), 8), :].astype(BF16)
        out_ref[j, 0] = rows[0:4]
        out_ref[j, 1] = rows[4:8]
        return carry

    lax.fori_loop(0, ALL_CHIPS, pack_step, 0, unroll=8)
    pl.semaphore_wait(barrier, ALL_CHIPS)
    exchange_start(0, out_ref, mid_ref)

    position = receive_positions(dest_ref)
    place = onehot(iota((ROWS, PACKED), 0).astype(F32) == position[0:1, :])
    loads[2].wait()
    loads[3].wait()
    g_ref[...] = mm_nt(og_ref[...], wo_ref[...]).astype(BF16)
    loads[4].wait()
    loads[5].wait()
    loads[6].wait()

    exchange_arrive(0, out_ref, mid_ref, over_ref)
    own_rows(mid_ref)
    hidden = mm(place[:, : PACKED // 2], rows_ref[: PACKED // 2].astype(BF16))
    over_rows(0, mid_ref, over_ref)
    hidden = hidden + mm(place[:, PACKED // 2 :], rows_ref[PACKED // 2 :].astype(BF16))
    hidden_ref[...] = hidden.astype(BF16)
    normalized, _ = normalize(hidden)
    gain = gain_ref[...].reshape(1, D)
    normed = (normalized * gain).astype(BF16)
    k_ref[...] = mm(normed, wk_ref[...]).astype(BF16)
    v_ref[...] = mm(normed, wv_ref[...]).astype(BF16)

    chosen = head_of_row()
    pick = onehot(iota((FAR, ROWS), 0) == iota((FAR, ROWS), 1) // 16)
    none = jnp.zeros((ROWS, D), BF16)
    own = chip_rows(chip)
    far_k = mm(pick, jnp.where(chosen, k_ref[...], none)).astype(BF16)
    far_v = mm(pick, jnp.where(chosen, v_ref[...], none)).astype(BF16)
    for c in range(PAIRS):
        far_ref[c, 0, own, 0:LANES] = far_k[:, c * LANES : (c + 1) * LANES]
        far_ref[c, 0, own, LANES:] = far_v[:, c * LANES : (c + 1) * LANES]

    def gather_copy(c, r):
        return pltpu.make_async_remote_copy(
            src_ref=far_ref.at[c, 0, own], dst_ref=far_ref.at[c, 0, own],
            send_sem=g_send.at[c], recv_sem=g_recv.at[c],
            device_id=same_core(ahead(r)), device_id_type=MESH,
        )

    def forward_copy(c):
        return pltpu.make_async_remote_copy(
            src_ref=far_ref.at[c, 0], dst_ref=far_ref.at[c, 1],
            send_sem=f_send.at[c], recv_sem=f_recv.at[c],
            device_id=partner, device_id_type=MESH,
        )

    def pass_on(c):
        fifteen = far_ref.at[c, 0, pl.ds(0, HALF - FAR)]
        pltpu.make_async_copy(fifteen, fifteen, g_recv.at[c]).wait()
        forward_copy(c).start()

    loop(0, PAIRS, lambda c: loop(1, CHIPS, lambda r: gather_copy(c, r).start()))
    q_ref[...] = mm(normed, wq_ref[...]).astype(BF16) * jnp.bfloat16(0.125)
    pass_on(0)

    def half_copy(c):
        return pltpu.make_async_remote_copy(
            src_ref=half_send.at[c], dst_ref=half_recv.at[c],
            send_sem=h_send.at[c], recv_sem=h_recv.at[c],
            device_id=partner, device_id_type=MESH,
        )

    def part_copy(c, r):
        other = ahead(r)
        return pltpu.make_async_remote_copy(
            src_ref=part_send.at[c, chip_rows(other)], dst_ref=part_recv.at[c, own],
            send_sem=p_send.at[c], recv_sem=p_recv.at[c],
            device_id=same_core(other), device_id_type=MESH,
        )

    def share(c):
        half_copy(c).wait_recv()
        part_send[c] = (keep_ref[c] + half_recv[c].astype(F32)).astype(BF16)
        part_recv[c, own] = part_send[c, own]
        loop(1, CHIPS, lambda r: part_copy(c, r).start())

    low = iota((ROWS, LANES), 1) < 64
    zero = jnp.zeros((ROWS, LANES), BF16)

    def both(pair):
        return jnp.concatenate([jnp.where(low, pair, zero), jnp.where(low, zero, pair)], axis=0)

    def mixed(near_t, far_t, near_w, far_w):
        first = mm(near_t[:64], near_w[:, :ROWS]) + mm(far_t[:64], far_w[:, :ROWS])
        second = mm(near_t[64:], near_w[:, ROWS:]) + mm(far_t[64:], far_w[:, ROWS:])
        return jnp.concatenate([first, second], axis=0).T

    def attend(c, carry):
        cols = pl.ds(pl.multiple_of(c * LANES, LANES), LANES)
        q2, g2 = both(q_ref[:, cols]), both(g_ref[:, cols])
        kn, vn = k_ref[:, cols], v_ref[:, cols]
        forward_copy(c).wait_recv()
        kf = far_ref[c, :, :, 0:LANES].reshape(2 * HALF, LANES)
        vf = far_ref[c, :, :, LANES:].reshape(2 * HALF, LANES)
        sn, sf = mm_nt(kn, q2), mm_nt(kf, q2)
        top = jnp.maximum(jnp.max(sn, axis=0, keepdims=True), jnp.max(sf, axis=0, keepdims=True))
        en, ef = jnp.exp(sn - top), jnp.exp(sf - top)
        inv = 1.0 / (jnp.sum(en, axis=0, keepdims=True) + jnp.sum(ef, axis=0, keepdims=True))
        pn, pf = en * inv, ef * inv
        wn, wf = pn.astype(BF16), pf.astype(BF16)
        dn, df = mm_nt(vn, g2), mm_nt(vf, g2)
        delta = jnp.sum(pn * dn, axis=0, keepdims=True) + jnp.sum(pf * df, axis=0, keepdims=True)
        tn, tf = (pn * (dn - delta)).astype(BF16), (pf * (df - delta)).astype(BF16)
        dkf, dvf = mm(tf, q2), mm(wf, g2)
        keep_ref[c, :, :LANES] = dkf[:HALF]
        keep_ref[c, :, LANES:] = dvf[:HALF]
        half_send[c, :, :LANES] = dkf[HALF:].astype(BF16)
        half_send[c, :, LANES:] = dvf[HALF:].astype(BF16)
        half_copy(c).start()

        @pl.when(c < PAIRS - 1)
        def _():
            pass_on(c + 1)

        dk_ref[:, cols] = mm(tn, q2)
        dv_ref[:, cols] = mm(wn, g2)
        att_ref[:, cols] = mixed(vn.T, vf.T, wn, wf).astype(BF16)
        dq_ref[:, cols] = (mixed(kn.T, kf.T, tn, tf) * 0.125).astype(BF16)

        @pl.when(c > 0)
        def _():
            share(c - 1)

        return carry

    lax.fori_loop(0, PAIRS, attend, 0)
    share(PAIRS - 1)

    hidden = hidden_ref[...].astype(F32)
    grad_normed = mm_nt(dq_ref[...], wq_ref[...])
    layer_ref[...] = (hidden + mm(att_ref[...], wo_ref[...])).astype(BF16)
    column = position.T[:, 0:1]
    unplace = onehot(iota((PACKED, ROWS), 1).astype(F32) == column)

    def add_far(c, carry):
        fifteen = pl.ds(0, HALF - FAR)
        pltpu.make_async_copy(part_send.at[c, fifteen], part_recv.at[c, fifteen], p_recv.at[c]).wait()
        cols = pl.ds(pl.multiple_of(c * LANES, LANES), LANES)
        total = jnp.sum(part_recv[c].astype(F32).reshape(CHIPS, FAR, 2 * LANES), axis=0)
        spread = jnp.broadcast_to(total[:, None, :], (FAR, 16, 2 * LANES)).reshape(ROWS, 2 * LANES)
        seen = iota((ROWS, LANES), 0) % 16 == iota((ROWS, LANES), 1) // 64 + 2 * c
        dk_ref[:, cols] += jnp.where(seen, spread[:, :LANES], 0.0)
        dv_ref[:, cols] += jnp.where(seen, spread[:, LANES:], 0.0)
        return carry

    lax.fori_loop(0, PAIRS, add_far, 0)

    grad_normed = grad_normed + mm_nt(dk_ref[...].astype(BF16), wk_ref[...])
    grad_normed = grad_normed + mm_nt(dv_ref[...].astype(BF16), wv_ref[...])
    normalized, inverse = normalize(hidden)
    scaled = grad_normed * gain
    inner = (
        scaled
        - jnp.mean(scaled, axis=1, keepdims=True)
        - normalized * jnp.mean(scaled * normalized, axis=1, keepdims=True)
    )
    grad_hidden = (og_ref[...].astype(F32) + inner * inverse).astype(BF16)

    rows_ref[...] = mm(unplace, grad_hidden)

    def unpack_step(i, carry):
        mine = rows_ref[pl.ds(pl.multiple_of(i * 8, 8), 8), :].astype(BF16)
        theirs = rows_ref[pl.ds(pl.multiple_of(PACKED // 2 + i * 8, 8), 8), :].astype(BF16)
        out2_ref[2 * i, core] = mine[0:4]
        out2_ref[2 * i + 1, core] = mine[4:8]
        out2_ref[2 * i, other_core] = theirs[0:4]
        out2_ref[2 * i + 1, other_core] = theirs[4:8]
        return carry

    lax.fori_loop(0, ALL_CHIPS // 2, unpack_step, 0, unroll=8)
    exchange_start(1, out2_ref, mid2_ref)

    exchange_sent(0, out_ref, mid_ref, over_ref)

    def sent(c):
        fifteen = far_ref.at[c, 0, pl.ds(0, HALF - FAR)]
        pltpu.make_async_copy(fifteen, fifteen, g_send.at[c]).wait()
        forward_copy(c).wait_send()
        half_copy(c).wait_send()
        parts = part_send.at[c, pl.ds(0, HALF - FAR)]
        pltpu.make_async_copy(parts, parts, p_send.at[c]).wait()

    loop(0, PAIRS, sent)

    exchange_arrive(1, out2_ref, mid2_ref, over2_ref)
    own_rows(mid2_ref)
    back = mm(pick_back[:, : PACKED // 2], rows_ref[: PACKED // 2].astype(BF16))
    over_rows(1, mid2_ref, over2_ref)
    back = back + mm(pick_back[:, PACKED // 2 :], rows_ref[PACKED // 2 :].astype(BF16))
    back_ref[...] = back.astype(BF16)
    exchange_sent(1, out2_ref, mid2_ref, over2_ref)


def per_device(tiles, dest_row, w_in, norm_gain, w_query, w_key, w_value, w_out, out_grad):
    vmem = pl.BlockSpec(memory_space=pltpu.VMEM)
    hbm = pl.BlockSpec(memory_space=pl.ANY)
    dma = pltpu.SemaphoreType.DMA
    slots = (ALL_CHIPS, 2, SLOTS, D)
    over = (ALL_CHIPS, SLOTS, D)
    pairs = (PAIRS, HALF, 2 * LANES)

    def bf16(*shape):
        return pltpu.VMEM(shape, BF16)

    def f32(*shape):
        return pltpu.VMEM(shape, F32)

    layer_out, grad_hidden = pl.pallas_call(
        block_kernel,
        out_shape=(jax.ShapeDtypeStruct((ROWS, D), BF16), jax.ShapeDtypeStruct((ROWS, D), BF16)),
        in_specs=[hbm, vmem, vmem] + [hbm] * 6,
        out_specs=(vmem, vmem),
        scratch_shapes=[
            bf16(ROWS, WIDTH), bf16(WIDTH, D), bf16(D, D), bf16(D, D), bf16(D, D), bf16(D, D), bf16(ROWS, D),
            f32(PACKED, D), bf16(*slots), bf16(*slots), bf16(*over), bf16(*slots), bf16(*slots), bf16(*over),
            bf16(ROWS, D), bf16(ROWS, D), bf16(ROWS, D), bf16(ROWS, D), bf16(ROWS, D),
            bf16(PAIRS, 2, HALF, 2 * LANES),
            bf16(ROWS, D), bf16(ROWS, D), f32(ROWS, D), f32(ROWS, D),
            f32(*pairs), bf16(*pairs), bf16(*pairs), bf16(*pairs), bf16(*pairs),
            dma((7,)), dma((2,)), dma((2, GROUPS)), dma((2, GROUPS)), dma((2, GROUPS)),
            dma((PAIRS,)), dma((PAIRS,)), dma((PAIRS,)), dma((PAIRS,)),
            dma((PAIRS,)), dma((PAIRS,)), dma((PAIRS,)), dma((PAIRS,)),
        ],
        compiler_params=pltpu.CompilerParams(
            vmem_limit_bytes=VMEM_LIMIT, collective_id=0, has_side_effects=True
        ),
    )(tiles, dest_row.reshape(ROWS, DEVICES), norm_gain, w_in, w_query, w_key, w_value, w_out, out_grad)
    return layer_out, mm_nt(grad_hidden, w_in).astype(BF16)


def solution(mesh):
    split = P(("slide", "seq"), None)
    return jax.shard_map(
        per_device,
        mesh=mesh,
        in_specs=(split, P(), P(), P(), P(), P(), P(), P(), split),
        out_specs=(split, split),
        check_vma=False,
    )
```

```python
import jax
import jax.numpy as jnp
from jax import lax
from jax.experimental import pallas as pl
from jax.experimental.pallas import tpu as pltpu
from jax.sharding import PartitionSpec as P

ROWS = 256
WIDTH = 1536
D = 768
DEVICES = 128
SLOTS = 4
PACKED = DEVICES * SLOTS
ALL_CHIPS = 64
GROUPS = 4
GROUP = ALL_CHIPS // GROUPS
MIX = 37
UNMIX = 45
CHIPS = 16
FAR = 16
HALF = CHIPS * FAR
PAIRS = 6
STRIP = 16
LANES = 128
MESH = pl.DeviceIdType.MESH
F32 = jnp.float32
BF16 = jnp.bfloat16
VMEM_LIMIT = 60 * 1024 * 1024


def mm(left, right):
    return jnp.dot(left, right, preferred_element_type=F32)


def mm_nt(left, right):
    return lax.dot_general(left, right, (((1,), (1,)), ((), ())), preferred_element_type=F32)


def iota(shape, dim):
    return lax.broadcasted_iota(jnp.int32, shape, dim)


def onehot(cond):
    return jnp.where(cond, 1.0, 0.0).astype(BF16)


def where_am_i():
    slide, seq = lax.axis_index("slide"), lax.axis_index("seq")
    return slide, seq // 8, (seq // 2) % 4, seq % 2


def message_of(device, sign):
    slide, z, y, core = where_am_i()
    by_slide = (sign * (device // 32 - slide)) & 3
    by_z = (sign * ((device // 8) % 4 - z)) & 3
    by_y = (sign * ((device // 2) % 4 - y)) & 3
    offset = by_slide * 16 + by_z * 4 + by_y
    return (offset * UNMIX) & 63, device % 2


def own_targets(dest_ref):
    slide, z, y, core = where_am_i()
    me = slide * 32 + z * 8 + y * 2 + core
    own = jnp.concatenate([dest_ref[pl.ds(2 * me, 1), :], dest_ref[pl.ds(2 * me + 1, 1), :]], axis=1)
    device = jnp.broadcast_to(own // ROWS, (ROWS, ROWS))
    target = device.astype(F32)
    across = target.T
    same = across == target
    before_row = iota((ROWS, ROWS), 0) < iota((ROWS, ROWS), 1)
    before_col = iota((ROWS, ROWS), 1) < iota((ROWS, ROWS), 0)
    rank_row = jnp.sum(jnp.where(same & before_row, 1.0, 0.0), axis=0, keepdims=True)
    rank_col = jnp.sum(jnp.where(same & before_col, 1.0, 0.0), axis=1, keepdims=True)
    row = message_of(device[0:1, :], 1)
    col = message_of(across[:, 0:1].astype(jnp.int32), 1)
    send_row = row[0] * 8 + row[1] * SLOTS + rank_row.astype(jnp.int32)
    back_col = (col[1] ^ core) * (PACKED // 2) + col[0] * SLOTS + rank_col.astype(jnp.int32)
    return send_row, back_col


def receive_positions(dest_ref):
    slide, z, y, core = where_am_i()
    me = slide * 32 + z * 8 + y * 2 + core
    half = ROWS // 2
    dest = dest_ref[...].astype(F32).T.astype(jnp.int32)
    mine = dest // ROWS == me
    marks = onehot(mine)
    before = onehot(iota((half, half), 1) < iota((half, half), 0))
    lane = iota((ROWS, ROWS), 1)
    first_half = onehot((iota((ROWS, ROWS), 0) == lane - 1) & (lane % 2 == 1))
    count = mm(jnp.ones((half, half), BF16), marks).astype(BF16)
    rank = mm(before, marks) + mm(count, first_half)
    place = jnp.where(mine, (dest % ROWS).astype(F32) + 1.0, 0.0)
    message, sender_core = message_of(iota((ROWS, 1), 0) // 2, -1)
    slot = (sender_core ^ core) * (PACKED // 2) + message * SLOTS
    column = iota((ROWS, PACKED), 1)
    total = jnp.zeros((8, PACKED), F32)
    for k in range(SLOTS):
        held = jnp.sum(jnp.where(rank == k, place, 0.0), axis=0, keepdims=True)
        total = total + mm(jnp.broadcast_to(held, (8, ROWS)).astype(BF16), onehot(column == slot + k))
    return total - 1.0


def head_of_row():
    return iota((ROWS, D), 0) % 16 == iota((ROWS, D), 1) // 64


def normalize(hidden):
    centre = jnp.mean(hidden, axis=1, keepdims=True)
    centered = hidden - centre
    spread = jnp.mean(centered * centered, axis=1, keepdims=True)
    inverse = lax.rsqrt(spread + 1e-05)
    return centered * inverse, inverse


def block_kernel(
    tiles_hbm, dest_ref, gain_ref, w_in_hbm, wq_hbm, wk_hbm, wv_hbm, wo_hbm, og_hbm,
    layer_ref, back_ref,
    tiles_ref, w_in_ref, wq_ref, wk_ref, wv_ref, wo_ref, og_ref,
    rows_ref, out_ref, mid_ref, over_ref, out2_ref, mid2_ref, over2_ref,
    hidden_ref, q_ref, k_ref, v_ref, g_ref, far_ref,
    att_ref, dq_ref, dk_ref, dv_ref,
    qg_ref, near_ref, stat_ref, scores_ref, work_ref, keep_ref, half_send, half_recv, part_send, part_recv,
    load_sem, x_send, x_recv, o_send, o_recv,
    g_send, g_recv, f_send, f_recv, h_send, h_recv, p_send, p_recv,
):
    slide, z, y, core = where_am_i()
    chip = z * 4 + y
    other_core = 1 - core
    partner = (slide, chip * 2 + other_core)

    def ahead(r):
        return ((z + r // 4) % 4) * 4 + (y + r % 4) % 4

    def same_core(other):
        return (slide, other * 2 + core)

    def chip_rows(other):
        return pl.ds(pl.multiple_of(other * FAR, FAR), FAR)

    def at_offset(offset):
        to_slide = (slide + offset // 16) % 4
        to_z = (z + (offset // 4) % 4) % 4
        to_y = (y + offset % 4) % 4
        return (to_slide, (to_z * 4 + to_y) * 2 + core)

    def loop(first, last, do):
        def step(i, carry):
            do(i)
            return carry

        lax.fori_loop(first, last, step, 0)

    loads = [
        pltpu.make_async_copy(source, target, load_sem.at[i])
        for i, (source, target) in enumerate(
            [
                (tiles_hbm, tiles_ref), (w_in_hbm, w_in_ref), (og_hbm, og_ref), (wo_hbm, wo_ref),
                (wk_hbm, wk_ref), (wv_hbm, wv_ref), (wq_hbm, wq_ref),
            ]
        )
    ]
    for load in loads:
        load.start()

    barrier = pltpu.get_barrier_semaphore()

    def greet(j):
        device = at_offset((j * MIX) & 63)
        pl.semaphore_signal(barrier, inc=1, device_id=device, device_id_type=MESH)

    loop(1, ALL_CHIPS, greet)
    pl.semaphore_signal(barrier, inc=1, device_id=partner, device_id_type=MESH)

    def message(way, j, source, landing):
        offset = (j * MIX) & 63
        device = at_offset(offset) if way == 0 else at_offset(
            ((4 - offset // 16) % 4) * 16 + ((4 - (offset // 4) % 4) % 4) * 4 + (4 - offset % 4) % 4
        )
        return pltpu.make_async_remote_copy(
            src_ref=source.at[j], dst_ref=landing.at[j],
            send_sem=x_send.at[way], recv_sem=x_recv.at[way, j // GROUP],
            device_id=device, device_id_type=MESH,
        )

    def hand_over(way, group, landing, over):
        part = pl.ds(group * GROUP, GROUP)
        return pltpu.make_async_remote_copy(
            src_ref=landing.at[part, other_core], dst_ref=over.at[part],
            send_sem=o_send.at[way, group], recv_sem=o_recv.at[way, group],
            device_id=partner, device_id_type=MESH,
        )

    def exchange_start(way, source, landing):
        loop(1, ALL_CHIPS, lambda j: message(way, j, source, landing).start())
        landing[0] = source[0]

    def exchange_arrive(way, source, landing, over):
        for group in range(GROUPS):
            arrived = pl.ds(group * GROUP + (group == 0), GROUP - (group == 0))
            pltpu.make_async_copy(source.at[arrived], landing.at[arrived], x_recv.at[way, group]).wait()
            hand_over(way, group, landing, over).start()

    def own_rows(landing):
        def step(i, carry):
            first = landing[2 * i, core].astype(F32)
            second = landing[2 * i + 1, core].astype(F32)
            rows_ref[pl.ds(pl.multiple_of(i * 8, 8), 8), :] = jnp.concatenate([first, second], axis=0)
            return carry

        lax.fori_loop(0, ALL_CHIPS // 2, step, 0, unroll=8)

    def over_rows(way, landing, over):
        for group in range(GROUPS):
            hand_over(way, group, landing, over).wait_recv()

        def step(i, carry):
            first = over[2 * i].astype(F32)
            second = over[2 * i + 1].astype(F32)
            start = pl.multiple_of(PACKED // 2 + i * 8, 8)
            rows_ref[pl.ds(start, 8), :] = jnp.concatenate([first, second], axis=0)
            return carry

        lax.fori_loop(0, ALL_CHIPS // 2, step, 0, unroll=8)

    def exchange_sent(way, source, landing, over):
        left = pl.ds(1, ALL_CHIPS - 1)
        pltpu.make_async_copy(source.at[left], landing.at[left], x_send.at[way]).wait()
        for group in range(GROUPS):
            hand_over(way, group, landing, over).wait_send()

    send_row, back_col = own_targets(dest_ref)
    pack = onehot(iota((PACKED, ROWS), 0) == send_row)
    pick_back = onehot(iota((ROWS, PACKED), 1) == back_col)
    loads[0].wait()
    loads[1].wait()
    rows_ref[...] = mm(pack, mm(tiles_ref[...], w_in_ref[...]).astype(BF16))

    def pack_step(j, carry):
        rows = rows_ref[pl.ds(pl.multiple_of(j * 8, 8), 8), :].astype(BF16)
        out_ref[j, 0] = rows[0:4]
        out_ref[j, 1] = rows[4:8]
        return carry

    lax.fori_loop(0, ALL_CHIPS, pack_step, 0, unroll=8)
    pl.semaphore_wait(barrier, ALL_CHIPS)
    exchange_start(0, out_ref, mid_ref)

    position = receive_positions(dest_ref)
    place = onehot(iota((ROWS, PACKED), 0).astype(F32) == position[0:1, :])
    loads[2].wait()
    loads[3].wait()
    g_ref[...] = mm_nt(og_ref[...], wo_ref[...]).astype(BF16)
    loads[4].wait()
    loads[5].wait()
    loads[6].wait()

    exchange_arrive(0, out_ref, mid_ref, over_ref)
    own_rows(mid_ref)
    hidden = mm(place[:, : PACKED // 2], rows_ref[: PACKED // 2].astype(BF16))
    over_rows(0, mid_ref, over_ref)
    hidden = hidden + mm(place[:, PACKED // 2 :], rows_ref[PACKED // 2 :].astype(BF16))
    hidden_ref[...] = hidden.astype(BF16)
    normalized, _ = normalize(hidden)
    gain = gain_ref[...].reshape(1, D)
    normed = (normalized * gain).astype(BF16)
    k_ref[...] = mm(normed, wk_ref[...]).astype(BF16)
    v_ref[...] = mm(normed, wv_ref[...]).astype(BF16)

    chosen = head_of_row()
    pick = onehot(iota((FAR, ROWS), 0) == iota((FAR, ROWS), 1) // 16)
    none = jnp.zeros((ROWS, D), BF16)
    own = chip_rows(chip)
    far_k = mm(pick, jnp.where(chosen, k_ref[...], none)).astype(BF16)
    far_v = mm(pick, jnp.where(chosen, v_ref[...], none)).astype(BF16)
    for c in range(PAIRS):
        far_ref[c, 0, own, 0:LANES] = far_k[:, c * LANES : (c + 1) * LANES]
        far_ref[c, 0, own, LANES:] = far_v[:, c * LANES : (c + 1) * LANES]

    def gather_copy(c, r):
        return pltpu.make_async_remote_copy(
            src_ref=far_ref.at[c, 0, own], dst_ref=far_ref.at[c, 0, own],
            send_sem=g_send.at[c], recv_sem=g_recv.at[c],
            device_id=same_core(ahead(r)), device_id_type=MESH,
        )

    def forward_copy(c):
        return pltpu.make_async_remote_copy(
            src_ref=far_ref.at[c, 0], dst_ref=far_ref.at[c, 1],
            send_sem=f_send.at[c], recv_sem=f_recv.at[c],
            device_id=partner, device_id_type=MESH,
        )

    def pass_on(c):
        fifteen = far_ref.at[c, 0, pl.ds(0, HALF - FAR)]
        pltpu.make_async_copy(fifteen, fifteen, g_recv.at[c]).wait()
        forward_copy(c).start()

    loop(0, PAIRS, lambda c: loop(1, CHIPS, lambda r: gather_copy(c, r).start()))
    q_ref[...] = mm(normed, wq_ref[...]).astype(BF16) * jnp.bfloat16(0.125)

    low = iota((ROWS, LANES), 1) < 64
    zero = jnp.zeros((ROWS, LANES), BF16)
    wide = 2 * ROWS

    def near(c):
        cols = pl.ds(pl.multiple_of(c * LANES, LANES), LANES)
        for first, pair in ((0, q_ref[:, cols]), (wide, g_ref[:, cols])):
            qg_ref[c, first : first + ROWS] = jnp.where(low, pair, zero)
            qg_ref[c, first + ROWS : first + wide] = jnp.where(low, zero, pair)
        near_ref[c, :, :wide] = mm_nt(k_ref[:, cols], qg_ref[c, :wide])
        near_ref[c, :, wide:] = mm_nt(v_ref[:, cols], qg_ref[c, wide:])
        top, total, inner = grow(near_ref.at[c], ROWS)
        stat_ref[c, 0:1] = top
        stat_ref[c, 1:2] = total
        stat_ref[c, 2:3] = inner

    def grow(matrix, count):
        strips = [slice(i, i + STRIP) for i in range(0, count, STRIP)]
        top = matrix[strips[0], :wide]
        for strip in strips[1:]:
            top = jnp.maximum(top, matrix[strip, :wide])
        top = jnp.max(top, axis=0, keepdims=True)
        total = jnp.zeros((STRIP, wide), F32)
        inner = jnp.zeros((STRIP, wide), F32)
        for strip in strips:
            grown = jnp.exp(matrix[strip, :wide] - top)
            matrix[strip, :wide] = grown
            total = total + grown
            inner = inner + grown * matrix[strip, wide:]
        return top, jnp.sum(total, axis=0, keepdims=True), jnp.sum(inner, axis=0, keepdims=True)

    def shrink(c, matrix, first, count, factor, delta):
        for i in range(0, count, STRIP):
            prob = matrix[i : i + STRIP, :wide] * factor
            out = slice(first + i, first + i + STRIP)
            work_ref[c, out, :wide] = (prob * (matrix[i : i + STRIP, wide:] - delta)).astype(BF16)
            work_ref[c, out, wide:] = prob.astype(BF16)

    loop(0, PAIRS, near)
    pass_on(0)

    def half_copy(c):
        return pltpu.make_async_remote_copy(
            src_ref=half_send.at[c], dst_ref=half_recv.at[c],
            send_sem=h_send.at[c], recv_sem=h_recv.at[c],
            device_id=partner, device_id_type=MESH,
        )

    def part_copy(c, r):
        other = ahead(r)
        return pltpu.make_async_remote_copy(
            src_ref=part_send.at[c, chip_rows(other)], dst_ref=part_recv.at[c, own],
            send_sem=p_send.at[c], recv_sem=p_recv.at[c],
            device_id=same_core(other), device_id_type=MESH,
        )

    def share(c):
        half_copy(c).wait_recv()
        part_send[c] = (keep_ref[c] + half_recv[c].astype(F32)).astype(BF16)
        part_recv[c, own] = part_send[c, own]
        loop(1, CHIPS, lambda r: part_copy(c, r).start())

    def mixed(near_t, far_t, near_w, far_w):
        first = mm(near_t[:64], near_w[:, :ROWS]) + mm(far_t[:64], far_w[:, :ROWS])
        second = mm(near_t[64:], near_w[:, ROWS:]) + mm(far_t[64:], far_w[:, ROWS:])
        return jnp.concatenate([first, second], axis=0).T

    def attend(c):
        forward_copy(c).wait_recv()

        @pl.when(c < PAIRS - 1)
        def _():
            pass_on(c + 1)

        q2, g2 = qg_ref[c, :wide], qg_ref[c, wide:]
        scores_ref[:, :wide] = mm_nt(far_ref[c, :, :, 0:LANES].reshape(2 * HALF, LANES), q2)
        scores_ref[:, wide:] = mm_nt(far_ref[c, :, :, LANES:].reshape(2 * HALF, LANES), g2)
        top, total, inner = grow(scores_ref, 2 * HALF)
        near_top = stat_ref[c, 0:1]
        joint = jnp.maximum(top, near_top)
        near_part, far_part = jnp.exp(near_top - joint), jnp.exp(top - joint)
        inv = 1.0 / (near_part * stat_ref[c, 1:2] + far_part * total)
        delta = (near_part * stat_ref[c, 2:3] + far_part * inner) * inv
        stat_ref[c, 3:4] = near_part * inv
        stat_ref[c, 4:5] = delta
        shrink(c, scores_ref, ROWS, 2 * HALF, far_part * inv, delta)
        far_k_sum = mm(work_ref[c, ROWS:, :wide], q2)
        far_v_sum = mm(work_ref[c, ROWS:, wide:], g2)
        keep_ref[c, :, :LANES] = far_k_sum[:HALF]
        keep_ref[c, :, LANES:] = far_v_sum[:HALF]
        half_send[c, :, :LANES] = far_k_sum[HALF:].astype(BF16)
        half_send[c, :, LANES:] = far_v_sum[HALF:].astype(BF16)
        half_copy(c).start()

        @pl.when(c > 0)
        def _():
            share(c - 1)

    def gather_up(c):
        cols = pl.ds(pl.multiple_of(c * LANES, LANES), LANES)
        shrink(c, near_ref.at[c], 0, ROWS, stat_ref[c, 3:4], stat_ref[c, 4:5])
        dk_ref[:, cols] = mm(work_ref[c, :ROWS, :wide], qg_ref[c, :wide])
        dv_ref[:, cols] = mm(work_ref[c, :ROWS, wide:], qg_ref[c, wide:])
        kf = far_ref[c, :, :, 0:LANES].reshape(2 * HALF, LANES)
        vf = far_ref[c, :, :, LANES:].reshape(2 * HALF, LANES)
        weights, slopes = work_ref[c, :, wide:], work_ref[c, :, :wide]
        att_ref[:, cols] = mixed(v_ref[:, cols].T, vf.T, weights[:ROWS], weights[ROWS:]).astype(BF16)
        dq_ref[:, cols] = (mixed(k_ref[:, cols].T, kf.T, slopes[:ROWS], slopes[ROWS:]) * 0.125).astype(BF16)

        @pl.when(c == 0)
        def _():
            share(PAIRS - 1)

    loop(0, PAIRS, attend)
    loop(0, PAIRS, gather_up)

    hidden = hidden_ref[...].astype(F32)
    grad_normed = mm_nt(dq_ref[...], wq_ref[...])
    layer_ref[...] = (hidden + mm(att_ref[...], wo_ref[...])).astype(BF16)
    column = position.T[:, 0:1]
    unplace = onehot(iota((PACKED, ROWS), 1).astype(F32) == column)

    def add_far(c, carry):
        fifteen = pl.ds(0, HALF - FAR)
        pltpu.make_async_copy(part_send.at[c, fifteen], part_recv.at[c, fifteen], p_recv.at[c]).wait()
        cols = pl.ds(pl.multiple_of(c * LANES, LANES), LANES)
        total = jnp.sum(part_recv[c].astype(F32).reshape(CHIPS, FAR, 2 * LANES), axis=0)
        spread = jnp.broadcast_to(total[:, None, :], (FAR, 16, 2 * LANES)).reshape(ROWS, 2 * LANES)
        seen = iota((ROWS, LANES), 0) % 16 == iota((ROWS, LANES), 1) // 64 + 2 * c
        dk_ref[:, cols] += jnp.where(seen, spread[:, :LANES], 0.0)
        dv_ref[:, cols] += jnp.where(seen, spread[:, LANES:], 0.0)
        return carry

    lax.fori_loop(0, PAIRS, add_far, 0)

    grad_normed = grad_normed + mm_nt(dk_ref[...].astype(BF16), wk_ref[...])
    grad_normed = grad_normed + mm_nt(dv_ref[...].astype(BF16), wv_ref[...])
    normalized, inverse = normalize(hidden)
    scaled = grad_normed * gain
    inner = (
        scaled
        - jnp.mean(scaled, axis=1, keepdims=True)
        - normalized * jnp.mean(scaled * normalized, axis=1, keepdims=True)
    )
    grad_hidden = (og_ref[...].astype(F32) + inner * inverse).astype(BF16)

    rows_ref[...] = mm(unplace, grad_hidden)

    def unpack_step(i, carry):
        mine = rows_ref[pl.ds(pl.multiple_of(i * 8, 8), 8), :].astype(BF16)
        theirs = rows_ref[pl.ds(pl.multiple_of(PACKED // 2 + i * 8, 8), 8), :].astype(BF16)
        out2_ref[2 * i, core] = mine[0:4]
        out2_ref[2 * i + 1, core] = mine[4:8]
        out2_ref[2 * i, other_core] = theirs[0:4]
        out2_ref[2 * i + 1, other_core] = theirs[4:8]
        return carry

    lax.fori_loop(0, ALL_CHIPS // 2, unpack_step, 0, unroll=8)
    exchange_start(1, out2_ref, mid2_ref)

    exchange_sent(0, out_ref, mid_ref, over_ref)

    def sent(c):
        fifteen = far_ref.at[c, 0, pl.ds(0, HALF - FAR)]
        pltpu.make_async_copy(fifteen, fifteen, g_send.at[c]).wait()
        forward_copy(c).wait_send()
        half_copy(c).wait_send()
        parts = part_send.at[c, pl.ds(0, HALF - FAR)]
        pltpu.make_async_copy(parts, parts, p_send.at[c]).wait()

    loop(0, PAIRS, sent)

    exchange_arrive(1, out2_ref, mid2_ref, over2_ref)
    own_rows(mid2_ref)
    back = mm(pick_back[:, : PACKED // 2], rows_ref[: PACKED // 2].astype(BF16))
    over_rows(1, mid2_ref, over2_ref)
    back = back + mm(pick_back[:, PACKED // 2 :], rows_ref[PACKED // 2 :].astype(BF16))
    back_ref[...] = back.astype(BF16)
    exchange_sent(1, out2_ref, mid2_ref, over2_ref)


def per_device(tiles, dest_row, w_in, norm_gain, w_query, w_key, w_value, w_out, out_grad):
    vmem = pl.BlockSpec(memory_space=pltpu.VMEM)
    hbm = pl.BlockSpec(memory_space=pl.ANY)
    dma = pltpu.SemaphoreType.DMA
    slots = (ALL_CHIPS, 2, SLOTS, D)
    over = (ALL_CHIPS, SLOTS, D)
    pairs = (PAIRS, HALF, 2 * LANES)

    def bf16(*shape):
        return pltpu.VMEM(shape, BF16)

    def f32(*shape):
        return pltpu.VMEM(shape, F32)

    layer, grad_hidden = pl.pallas_call(
        block_kernel,
        out_shape=(jax.ShapeDtypeStruct((ROWS, D), BF16), jax.ShapeDtypeStruct((ROWS, D), BF16)),
        in_specs=[hbm, vmem, vmem] + [hbm] * 6,
        out_specs=(vmem, vmem),
        scratch_shapes=[
            bf16(ROWS, WIDTH), bf16(WIDTH, D), bf16(D, D), bf16(D, D), bf16(D, D), bf16(D, D), bf16(ROWS, D),
            f32(PACKED, D), bf16(*slots), bf16(*slots), bf16(*over), bf16(*slots), bf16(*slots), bf16(*over),
            bf16(ROWS, D), bf16(ROWS, D), bf16(ROWS, D), bf16(ROWS, D), bf16(ROWS, D),
            bf16(PAIRS, 2, HALF, 2 * LANES),
            bf16(ROWS, D), bf16(ROWS, D), f32(ROWS, D), f32(ROWS, D),
            bf16(PAIRS, 4 * ROWS, LANES), f32(PAIRS, ROWS, 4 * ROWS), f32(PAIRS, 8, 2 * ROWS),
            f32(2 * HALF, 4 * ROWS), bf16(PAIRS, ROWS + 2 * HALF, 4 * ROWS),
            f32(*pairs), bf16(*pairs), bf16(*pairs), bf16(*pairs), bf16(*pairs),
            dma((7,)), dma((2,)), dma((2, GROUPS)), dma((2, GROUPS)), dma((2, GROUPS)),
            dma((PAIRS,)), dma((PAIRS,)), dma((PAIRS,)), dma((PAIRS,)),
            dma((PAIRS,)), dma((PAIRS,)), dma((PAIRS,)), dma((PAIRS,)),
        ],
        compiler_params=pltpu.CompilerParams(
            vmem_limit_bytes=VMEM_LIMIT, collective_id=0, has_side_effects=True
        ),
    )(tiles, dest_row.reshape(ROWS, DEVICES), norm_gain, w_in, w_query, w_key, w_value, w_out, out_grad)
    return layer, mm_nt(grad_hidden, w_in).astype(BF16)


def solution(mesh):
    split = P(("slide", "seq"), None)
    return jax.shard_map(
        per_device,
        mesh=mesh,
        in_specs=(split, P(), P(), P(), P(), P(), P(), P(), split),
        out_specs=(split, split),
        check_vma=False,
    )
```

```python
import jax
import jax.numpy as jnp
from jax import lax
from jax.experimental import pallas as pl
from jax.experimental.pallas import tpu as pltpu
from jax.sharding import PartitionSpec as P

ROWS = 256
WIDTH = 1536
D = 768
DEVICES = 128
SLOTS = 4
PACKED = DEVICES * SLOTS
ALL_CHIPS = 64
GROUPS = 4
GROUP = ALL_CHIPS // GROUPS
MIX = 37
UNMIX = 45
CHIPS = 16
FAR_FIRST = (10, 9, 11, 6, 14, 2, 8, 5, 7, 13, 15, 1, 3, 4, 12)
FAR = 16
HALF = CHIPS * FAR
PAIRS = 6
STRIP = 16
LANES = 128
MESH = pl.DeviceIdType.MESH
F32 = jnp.float32
BF16 = jnp.bfloat16
VMEM_LIMIT = 60 * 1024 * 1024


def mm(left, right):
    return jnp.dot(left, right, preferred_element_type=F32)


def mm_nt(left, right):
    return lax.dot_general(left, right, (((1,), (1,)), ((), ())), preferred_element_type=F32)


def iota(shape, dim):
    return lax.broadcasted_iota(jnp.int32, shape, dim)


def onehot(cond):
    return jnp.where(cond, 1.0, 0.0).astype(BF16)


def where_am_i():
    slide, seq = lax.axis_index("slide"), lax.axis_index("seq")
    return slide, seq // 8, (seq // 2) % 4, seq % 2


def message_of(device, sign):
    slide, z, y, core = where_am_i()
    by_slide = (sign * (device // 32 - slide)) & 3
    by_z = (sign * ((device // 8) % 4 - z)) & 3
    by_y = (sign * ((device // 2) % 4 - y)) & 3
    offset = by_slide * 16 + by_z * 4 + by_y
    return (offset * UNMIX) & 63, device % 2


def own_targets(dest_ref):
    slide, z, y, core = where_am_i()
    me = slide * 32 + z * 8 + y * 2 + core
    own = jnp.concatenate([dest_ref[pl.ds(2 * me, 1), :], dest_ref[pl.ds(2 * me + 1, 1), :]], axis=1)
    device = jnp.broadcast_to(own // ROWS, (ROWS, ROWS))
    target = device.astype(F32)
    across = target.T
    same = across == target
    before_row = iota((ROWS, ROWS), 0) < iota((ROWS, ROWS), 1)
    before_col = iota((ROWS, ROWS), 1) < iota((ROWS, ROWS), 0)
    rank_row = jnp.sum(jnp.where(same & before_row, 1.0, 0.0), axis=0, keepdims=True)
    rank_col = jnp.sum(jnp.where(same & before_col, 1.0, 0.0), axis=1, keepdims=True)
    row = message_of(device[0:1, :], 1)
    col = message_of(across[:, 0:1].astype(jnp.int32), 1)
    send_row = row[0] * 8 + row[1] * SLOTS + rank_row.astype(jnp.int32)
    back_col = (col[1] ^ core) * (PACKED // 2) + col[0] * SLOTS + rank_col.astype(jnp.int32)
    return send_row, back_col


def receive_positions(dest_ref):
    slide, z, y, core = where_am_i()
    me = slide * 32 + z * 8 + y * 2 + core
    half = ROWS // 2
    dest = dest_ref[...].astype(F32).T.astype(jnp.int32)
    mine = dest // ROWS == me
    marks = onehot(mine)
    before = onehot(iota((half, half), 1) < iota((half, half), 0))
    lane = iota((ROWS, ROWS), 1)
    first_half = onehot((iota((ROWS, ROWS), 0) == lane - 1) & (lane % 2 == 1))
    count = mm(jnp.ones((half, half), BF16), marks).astype(BF16)
    rank = mm(before, marks) + mm(count, first_half)
    place = jnp.where(mine, (dest % ROWS).astype(F32) + 1.0, 0.0)
    message, sender_core = message_of(iota((ROWS, 1), 0) // 2, -1)
    slot = (sender_core ^ core) * (PACKED // 2) + message * SLOTS
    column = iota((ROWS, PACKED), 1)
    total = jnp.zeros((8, PACKED), F32)
    for k in range(SLOTS):
        held = jnp.sum(jnp.where(rank == k, place, 0.0), axis=0, keepdims=True)
        total = total + mm(jnp.broadcast_to(held, (8, ROWS)).astype(BF16), onehot(column == slot + k))
    return total - 1.0


def head_of_row():
    return iota((ROWS, D), 0) % 16 == iota((ROWS, D), 1) // 64


def normalize(hidden):
    centre = jnp.mean(hidden, axis=1, keepdims=True)
    centered = hidden - centre
    spread = jnp.mean(centered * centered, axis=1, keepdims=True)
    inverse = lax.rsqrt(spread + 1e-05)
    return centered * inverse, inverse


def block_kernel(
    tiles_hbm, dest_ref, gain_ref, w_in_hbm, wq_hbm, wk_hbm, wv_hbm, wo_hbm, og_hbm,
    layer_ref, back_ref,
    tiles_ref, w_in_ref, wq_ref, wk_ref, wv_ref, wo_ref, og_ref,
    rows_ref, out_ref, mid_ref, over_ref, out2_ref, mid2_ref, over2_ref,
    hidden_ref, q_ref, k_ref, v_ref, g_ref, far_ref,
    att_ref, dq_ref, dk_ref, dv_ref,
    qg_ref, near_ref, stat_ref, scores_ref, work_ref, keep_ref, half_send, half_recv, part_send, part_recv,
    load_sem, x_send, x_recv, o_send, o_recv,
    g_send, g_recv, f_send, f_recv, h_send, h_recv, p_send, p_recv,
):
    slide, z, y, core = where_am_i()
    chip = z * 4 + y
    other_core = 1 - core
    partner = (slide, chip * 2 + other_core)

    def ahead(r):
        return ((z + r // 4) % 4) * 4 + (y + r % 4) % 4

    def same_core(other):
        return (slide, other * 2 + core)

    def chip_rows(other):
        return pl.ds(pl.multiple_of(other * FAR, FAR), FAR)

    def at_offset(offset):
        to_slide = (slide + offset // 16) % 4
        to_z = (z + (offset // 4) % 4) % 4
        to_y = (y + offset % 4) % 4
        return (to_slide, (to_z * 4 + to_y) * 2 + core)

    def loop(first, last, do):
        def step(i, carry):
            do(i)
            return carry

        lax.fori_loop(first, last, step, 0)

    loads = [
        pltpu.make_async_copy(source, target, load_sem.at[i])
        for i, (source, target) in enumerate(
            [
                (tiles_hbm, tiles_ref), (w_in_hbm, w_in_ref), (og_hbm, og_ref), (wo_hbm, wo_ref),
                (wk_hbm, wk_ref), (wv_hbm, wv_ref), (wq_hbm, wq_ref),
            ]
        )
    ]
    for load in loads[:2]:
        load.start()

    barrier = pltpu.get_barrier_semaphore()

    def greet(j):
        device = at_offset((j * MIX) & 63)
        pl.semaphore_signal(barrier, inc=1, device_id=device, device_id_type=MESH)

    loop(1, ALL_CHIPS, greet)
    pl.semaphore_signal(barrier, inc=1, device_id=partner, device_id_type=MESH)

    def message(way, j, source, landing):
        offset = (j * MIX) & 63
        device = at_offset(offset) if way == 0 else at_offset(
            ((4 - offset // 16) % 4) * 16 + ((4 - (offset // 4) % 4) % 4) * 4 + (4 - offset % 4) % 4
        )
        return pltpu.make_async_remote_copy(
            src_ref=source.at[j], dst_ref=landing.at[j],
            send_sem=x_send.at[way], recv_sem=x_recv.at[way, j // GROUP],
            device_id=device, device_id_type=MESH,
        )

    def hand_over(way, group, landing, over):
        part = pl.ds(group * GROUP, GROUP)
        return pltpu.make_async_remote_copy(
            src_ref=landing.at[part, other_core], dst_ref=over.at[part],
            send_sem=o_send.at[way, group], recv_sem=o_recv.at[way, group],
            device_id=partner, device_id_type=MESH,
        )

    def exchange_start(way, source, landing, pack_step):
        for group in range(GROUPS):
            first = group * GROUP
            pack_step(first, first + GROUP)
            if way == 0 and group == 0:
                pl.semaphore_wait(barrier, ALL_CHIPS)
            loop(max(first, 1), first + GROUP, lambda j: message(way, j, source, landing).start())
        landing[0] = source[0]

    def to_rows(group, first_row, chunk):
        def step(i, carry):
            rows = jnp.concatenate([chunk(2 * i).astype(F32), chunk(2 * i + 1).astype(F32)], axis=0)
            rows_ref[pl.ds(pl.multiple_of(first_row + i * 8, 8), 8), :] = rows
            return carry

        lax.fori_loop(group * GROUP // 2, (group + 1) * GROUP // 2, step, 0, unroll=8)

    def exchange_arrive(way, source, landing, over):
        for group in range(GROUPS):
            arrived = pl.ds(group * GROUP + (group == 0), GROUP - (group == 0))
            pltpu.make_async_copy(source.at[arrived], landing.at[arrived], x_recv.at[way, group]).wait()
            hand_over(way, group, landing, over).start()
            to_rows(group, 0, lambda j: landing[j, core])

    def over_rows(way, landing, over):
        for group in range(GROUPS):
            hand_over(way, group, landing, over).wait_recv()
            to_rows(group, PACKED // 2, lambda j: over[j])

    def exchange_sent(way, source, landing, over):
        left = pl.ds(1, ALL_CHIPS - 1)
        pltpu.make_async_copy(source.at[left], landing.at[left], x_send.at[way]).wait()
        for group in range(GROUPS):
            hand_over(way, group, landing, over).wait_send()

    send_row, back_col = own_targets(dest_ref)
    pack = onehot(iota((PACKED, ROWS), 0) == send_row)
    pick_back = onehot(iota((ROWS, PACKED), 1) == back_col)
    loads[0].wait()
    loads[1].wait()
    for load in loads[2:]:
        load.start()
    rows_ref[...] = mm(pack, mm(tiles_ref[...], w_in_ref[...]).astype(BF16))

    def pack_send(first, last):
        def step(j, carry):
            rows = rows_ref[pl.ds(pl.multiple_of(j * 8, 8), 8), :].astype(BF16)
            out_ref[j, 0] = rows[0:4]
            out_ref[j, 1] = rows[4:8]
            return carry

        lax.fori_loop(first, last, step, 0, unroll=8)

    exchange_start(0, out_ref, mid_ref, pack_send)

    position = receive_positions(dest_ref)
    place = onehot(iota((ROWS, PACKED), 0).astype(F32) == position[0:1, :])
    loads[2].wait()
    loads[3].wait()
    g_ref[...] = mm_nt(og_ref[...], wo_ref[...]).astype(BF16)
    loads[4].wait()
    loads[5].wait()
    loads[6].wait()

    exchange_arrive(0, out_ref, mid_ref, over_ref)
    hidden = mm(place[:, : PACKED // 2], rows_ref[: PACKED // 2].astype(BF16))
    over_rows(0, mid_ref, over_ref)
    hidden = hidden + mm(place[:, PACKED // 2 :], rows_ref[PACKED // 2 :].astype(BF16))
    hidden_ref[...] = hidden.astype(BF16)
    normalized, _ = normalize(hidden)
    gain = gain_ref[...].reshape(1, D)
    normed = (normalized * gain).astype(BF16)
    k_ref[...] = mm(normed, wk_ref[...]).astype(BF16)
    v_ref[...] = mm(normed, wv_ref[...]).astype(BF16)

    chosen = head_of_row()
    pick = onehot(iota((FAR, ROWS), 0) == iota((FAR, ROWS), 1) // 16)
    none = jnp.zeros((ROWS, D), BF16)
    own = chip_rows(chip)
    far_k = mm(pick, jnp.where(chosen, k_ref[...], none)).astype(BF16)
    far_v = mm(pick, jnp.where(chosen, v_ref[...], none)).astype(BF16)
    for c in range(PAIRS):
        far_ref[c, 0, own, 0:LANES] = far_k[:, c * LANES : (c + 1) * LANES]
        far_ref[c, 0, own, LANES:] = far_v[:, c * LANES : (c + 1) * LANES]

    def gather_copy(c, r):
        return pltpu.make_async_remote_copy(
            src_ref=far_ref.at[c, 0, own], dst_ref=far_ref.at[c, 0, own],
            send_sem=g_send.at[c], recv_sem=g_recv.at[c],
            device_id=same_core(ahead(r)), device_id_type=MESH,
        )

    def forward_copy(c):
        return pltpu.make_async_remote_copy(
            src_ref=far_ref.at[c, 0], dst_ref=far_ref.at[c, 1],
            send_sem=f_send.at[c], recv_sem=f_recv.at[c],
            device_id=partner, device_id_type=MESH,
        )

    def pass_on(c):
        fifteen = far_ref.at[c, 0, pl.ds(0, HALF - FAR)]
        pltpu.make_async_copy(fifteen, fifteen, g_recv.at[c]).wait()
        forward_copy(c).start()

    def gather_start(c):
        for r in FAR_FIRST:
            gather_copy(c, r).start()

    loop(0, PAIRS, gather_start)
    q_ref[...] = mm(normed, wq_ref[...]).astype(BF16) * jnp.bfloat16(0.125)

    low = iota((ROWS, LANES), 1) < 64
    zero = jnp.zeros((ROWS, LANES), BF16)
    wide = 2 * ROWS

    def near(c):
        cols = pl.ds(pl.multiple_of(c * LANES, LANES), LANES)
        for first, pair in ((0, q_ref[:, cols]), (wide, g_ref[:, cols])):
            qg_ref[c, first : first + ROWS] = jnp.where(low, pair, zero)
            qg_ref[c, first + ROWS : first + wide] = jnp.where(low, zero, pair)
        near_ref[c, :, :wide] = mm_nt(k_ref[:, cols], qg_ref[c, :wide])
        near_ref[c, :, wide:] = mm_nt(v_ref[:, cols], qg_ref[c, wide:])
        top, total, inner = grow(near_ref.at[c], ROWS)
        stat_ref[c, 0:1] = top
        stat_ref[c, 1:2] = total
        stat_ref[c, 2:3] = inner

    def grow(matrix, count):
        strips = [slice(i, i + STRIP) for i in range(0, count, STRIP)]
        top = matrix[strips[0], :wide]
        for strip in strips[1:]:
            top = jnp.maximum(top, matrix[strip, :wide])
        top = jnp.max(top, axis=0, keepdims=True)
        total = jnp.zeros((STRIP, wide), F32)
        inner = jnp.zeros((STRIP, wide), F32)
        for strip in strips:
            grown = jnp.exp(matrix[strip, :wide] - top)
            matrix[strip, :wide] = grown
            total = total + grown
            inner = inner + grown * matrix[strip, wide:]
        return top, jnp.sum(total, axis=0, keepdims=True), jnp.sum(inner, axis=0, keepdims=True)

    def shrink(c, matrix, first, count, factor, delta):
        for i in range(0, count, STRIP):
            prob = matrix[i : i + STRIP, :wide] * factor
            out = slice(first + i, first + i + STRIP)
            work_ref[c, out, :wide] = (prob * (matrix[i : i + STRIP, wide:] - delta)).astype(BF16)
            work_ref[c, out, wide:] = prob.astype(BF16)

    loop(0, PAIRS, near)
    pass_on(0)

    def half_copy(c):
        return pltpu.make_async_remote_copy(
            src_ref=half_send.at[c], dst_ref=half_recv.at[c],
            send_sem=h_send.at[c], recv_sem=h_recv.at[c],
            device_id=partner, device_id_type=MESH,
        )

    def part_copy(c, r):
        other = ahead(r)
        return pltpu.make_async_remote_copy(
            src_ref=part_send.at[c, chip_rows(other)], dst_ref=part_recv.at[c, own],
            send_sem=p_send.at[c], recv_sem=p_recv.at[c],
            device_id=same_core(other), device_id_type=MESH,
        )

    def share(c):
        half_copy(c).wait_recv()
        part_send[c] = (keep_ref[c] + half_recv[c].astype(F32)).astype(BF16)
        part_recv[c, own] = part_send[c, own]
        for r in FAR_FIRST:
            part_copy(c, r).start()

    def mixed(near_t, far_t, near_w, far_w):
        first = mm(near_t[:64], near_w[:, :ROWS]) + mm(far_t[:64], far_w[:, :ROWS])
        second = mm(near_t[64:], near_w[:, ROWS:]) + mm(far_t[64:], far_w[:, ROWS:])
        return jnp.concatenate([first, second], axis=0).T

    def attend(c):
        forward_copy(c).wait_recv()

        @pl.when(c < PAIRS - 1)
        def _():
            pass_on(c + 1)

        q2, g2 = qg_ref[c, :wide], qg_ref[c, wide:]
        scores_ref[:, :wide] = mm_nt(far_ref[c, :, :, 0:LANES].reshape(2 * HALF, LANES), q2)
        scores_ref[:, wide:] = mm_nt(far_ref[c, :, :, LANES:].reshape(2 * HALF, LANES), g2)
        top, total, inner = grow(scores_ref, 2 * HALF)
        near_top = stat_ref[c, 0:1]
        joint = jnp.maximum(top, near_top)
        near_part, far_part = jnp.exp(near_top - joint), jnp.exp(top - joint)
        inv = 1.0 / (near_part * stat_ref[c, 1:2] + far_part * total)
        delta = (near_part * stat_ref[c, 2:3] + far_part * inner) * inv
        stat_ref[c, 3:4] = near_part * inv
        stat_ref[c, 4:5] = delta
        shrink(c, scores_ref, ROWS, 2 * HALF, far_part * inv, delta)
        far_k_sum = mm(work_ref[c, ROWS:, :wide], q2)
        far_v_sum = mm(work_ref[c, ROWS:, wide:], g2)
        keep_ref[c, :, :LANES] = far_k_sum[:HALF]
        keep_ref[c, :, LANES:] = far_v_sum[:HALF]
        half_send[c, :, :LANES] = far_k_sum[HALF:].astype(BF16)
        half_send[c, :, LANES:] = far_v_sum[HALF:].astype(BF16)
        half_copy(c).start()

        @pl.when(c > 0)
        def _():
            share(c - 1)

    def gather_up(c):
        cols = pl.ds(pl.multiple_of(c * LANES, LANES), LANES)
        shrink(c, near_ref.at[c], 0, ROWS, stat_ref[c, 3:4], stat_ref[c, 4:5])
        dk_ref[:, cols] = mm(work_ref[c, :ROWS, :wide], qg_ref[c, :wide])
        dv_ref[:, cols] = mm(work_ref[c, :ROWS, wide:], qg_ref[c, wide:])
        kf = far_ref[c, :, :, 0:LANES].reshape(2 * HALF, LANES)
        vf = far_ref[c, :, :, LANES:].reshape(2 * HALF, LANES)
        weights, slopes = work_ref[c, :, wide:], work_ref[c, :, :wide]
        att_ref[:, cols] = mixed(v_ref[:, cols].T, vf.T, weights[:ROWS], weights[ROWS:]).astype(BF16)
        dq_ref[:, cols] = (mixed(k_ref[:, cols].T, kf.T, slopes[:ROWS], slopes[ROWS:]) * 0.125).astype(BF16)

        @pl.when(c == 0)
        def _():
            share(PAIRS - 1)

    loop(0, PAIRS, attend)
    loop(0, PAIRS, gather_up)

    hidden = hidden_ref[...].astype(F32)
    grad_normed = mm_nt(dq_ref[...], wq_ref[...])
    layer_ref[...] = (hidden + mm(att_ref[...], wo_ref[...])).astype(BF16)
    column = position.T[:, 0:1]
    unplace = onehot(iota((PACKED, ROWS), 1).astype(F32) == column)

    def add_far(c, carry):
        fifteen = pl.ds(0, HALF - FAR)
        pltpu.make_async_copy(part_send.at[c, fifteen], part_recv.at[c, fifteen], p_recv.at[c]).wait()
        cols = pl.ds(pl.multiple_of(c * LANES, LANES), LANES)
        total = jnp.sum(part_recv[c].astype(F32).reshape(CHIPS, FAR, 2 * LANES), axis=0)
        spread = jnp.broadcast_to(total[:, None, :], (FAR, 16, 2 * LANES)).reshape(ROWS, 2 * LANES)
        seen = iota((ROWS, LANES), 0) % 16 == iota((ROWS, LANES), 1) // 64 + 2 * c
        dk_ref[:, cols] += jnp.where(seen, spread[:, :LANES], 0.0)
        dv_ref[:, cols] += jnp.where(seen, spread[:, LANES:], 0.0)
        return carry

    def project_back(cols):
        grads = jnp.concatenate([dk_ref[:, cols], dv_ref[:, cols]], axis=1).astype(BF16)
        return mm_nt(grads, jnp.concatenate([wk_ref[:, cols], wv_ref[:, cols]], axis=1))

    early = PAIRS - 2
    lax.fori_loop(0, early, add_far, 0)
    grad_normed = grad_normed + project_back(slice(0, early * LANES))
    lax.fori_loop(early, PAIRS, add_far, 0)
    grad_normed = grad_normed + project_back(slice(early * LANES, D))
    normalized, inverse = normalize(hidden)
    scaled = grad_normed * gain
    inner = (
        scaled
        - jnp.mean(scaled, axis=1, keepdims=True)
        - normalized * jnp.mean(scaled * normalized, axis=1, keepdims=True)
    )
    grad_hidden = (og_ref[...].astype(F32) + inner * inverse).astype(BF16)

    rows_ref[...] = mm(unplace, grad_hidden)

    def pack_back(first, last):
        def step(i, carry):
            mine = rows_ref[pl.ds(pl.multiple_of(i * 8, 8), 8), :].astype(BF16)
            theirs = rows_ref[pl.ds(pl.multiple_of(PACKED // 2 + i * 8, 8), 8), :].astype(BF16)
            out2_ref[2 * i, core] = mine[0:4]
            out2_ref[2 * i + 1, core] = mine[4:8]
            out2_ref[2 * i, other_core] = theirs[0:4]
            out2_ref[2 * i + 1, other_core] = theirs[4:8]
            return carry

        lax.fori_loop(first // 2, last // 2, step, 0, unroll=8)

    exchange_start(1, out2_ref, mid2_ref, pack_back)

    exchange_sent(0, out_ref, mid_ref, over_ref)

    def sent(c):
        fifteen = far_ref.at[c, 0, pl.ds(0, HALF - FAR)]
        pltpu.make_async_copy(fifteen, fifteen, g_send.at[c]).wait()
        forward_copy(c).wait_send()
        half_copy(c).wait_send()
        parts = part_send.at[c, pl.ds(0, HALF - FAR)]
        pltpu.make_async_copy(parts, parts, p_send.at[c]).wait()

    loop(0, PAIRS, sent)

    exchange_arrive(1, out2_ref, mid2_ref, over2_ref)
    back = mm(pick_back[:, : PACKED // 2], rows_ref[: PACKED // 2].astype(BF16))
    over_rows(1, mid2_ref, over2_ref)
    back = back + mm(pick_back[:, PACKED // 2 :], rows_ref[PACKED // 2 :].astype(BF16))
    back_ref[...] = back.astype(BF16)
    exchange_sent(1, out2_ref, mid2_ref, over2_ref)


def per_device(tiles, dest_row, w_in, norm_gain, w_query, w_key, w_value, w_out, out_grad):
    vmem = pl.BlockSpec(memory_space=pltpu.VMEM)
    hbm = pl.BlockSpec(memory_space=pl.ANY)
    dma = pltpu.SemaphoreType.DMA
    slots = (ALL_CHIPS, 2, SLOTS, D)
    over = (ALL_CHIPS, SLOTS, D)
    pairs = (PAIRS, HALF, 2 * LANES)

    def bf16(*shape):
        return pltpu.VMEM(shape, BF16)

    def f32(*shape):
        return pltpu.VMEM(shape, F32)

    layer, grad_hidden = pl.pallas_call(
        block_kernel,
        out_shape=(jax.ShapeDtypeStruct((ROWS, D), BF16), jax.ShapeDtypeStruct((ROWS, D), BF16)),
        in_specs=[hbm, vmem, vmem] + [hbm] * 6,
        out_specs=(vmem, vmem),
        scratch_shapes=[
            bf16(ROWS, WIDTH), bf16(WIDTH, D), bf16(D, D), bf16(D, D), bf16(D, D), bf16(D, D), bf16(ROWS, D),
            f32(PACKED, D), bf16(*slots), bf16(*slots), bf16(*over), bf16(*slots), bf16(*slots), bf16(*over),
            bf16(ROWS, D), bf16(ROWS, D), bf16(ROWS, D), bf16(ROWS, D), bf16(ROWS, D),
            bf16(PAIRS, 2, HALF, 2 * LANES),
            bf16(ROWS, D), bf16(ROWS, D), f32(ROWS, D), f32(ROWS, D),
            bf16(PAIRS, 4 * ROWS, LANES), f32(PAIRS, ROWS, 4 * ROWS), f32(PAIRS, 8, 2 * ROWS),
            f32(2 * HALF, 4 * ROWS), bf16(PAIRS, ROWS + 2 * HALF, 4 * ROWS),
            f32(*pairs), bf16(*pairs), bf16(*pairs), bf16(*pairs), bf16(*pairs),
            dma((7,)), dma((2,)), dma((2, GROUPS)), dma((2, GROUPS)), dma((2, GROUPS)),
            dma((PAIRS,)), dma((PAIRS,)), dma((PAIRS,)), dma((PAIRS,)),
            dma((PAIRS,)), dma((PAIRS,)), dma((PAIRS,)), dma((PAIRS,)),
        ],
        compiler_params=pltpu.CompilerParams(
            vmem_limit_bytes=VMEM_LIMIT, collective_id=0, has_side_effects=True
        ),
    )(tiles, dest_row.reshape(ROWS, DEVICES), norm_gain, w_in, w_query, w_key, w_value, w_out, out_grad)
    return layer, mm_nt(grad_hidden, w_in).astype(BF16)


def solution(mesh):
    split = P(("slide", "seq"), None)
    return jax.shard_map(
        per_device,
        mesh=mesh,
        in_specs=(split, P(), P(), P(), P(), P(), P(), P(), split),
        out_specs=(split, split),
        check_vma=False,
    )
```

```python
import jax
import jax.numpy as jnp
from jax import lax
from jax.experimental import pallas as pl
from jax.experimental.pallas import tpu as pltpu
from jax.sharding import PartitionSpec as P

ROWS = 256
WIDTH = 1536
D = 768
DEVICES = 128
SLOTS = 4
PACKED = DEVICES * SLOTS
ALL_CHIPS = 64
GROUPS = 4
GROUP = ALL_CHIPS // GROUPS
CHIPS = 16
FAR_FIRST = (10, 9, 11, 6, 14, 2, 8, 5, 7, 13, 15, 1, 3, 4, 12)
FAR = 16
HALF = CHIPS * FAR
PAIRS = 6
STRIP = 16
LANES = 128
MESH = pl.DeviceIdType.MESH


def hops(offset):
    return sum(min(part, 4 - part) for part in (offset // 16, offset // 4 % 4, offset % 4))


OFFSETS = [0] + sorted(range(1, ALL_CHIPS), key=lambda o: (-hops(o), o * 45 % 64))
F32 = jnp.float32
BF16 = jnp.bfloat16
VMEM_LIMIT = 60 * 1024 * 1024


def mm(left, right):
    return jnp.dot(left, right, preferred_element_type=F32)


def mm_nt(left, right):
    return lax.dot_general(left, right, (((1,), (1,)), ((), ())), preferred_element_type=F32)


def iota(shape, dim):
    return lax.broadcasted_iota(jnp.int32, shape, dim)


def onehot(cond):
    return jnp.where(cond, 1.0, 0.0).astype(BF16)


def where_am_i():
    slide, seq = lax.axis_index("slide"), lax.axis_index("seq")
    return slide, seq // 8, (seq // 2) % 4, seq % 2


def message_at(offset):
    down = 0 if offset.shape[0] == 1 else 1
    line = iota((ALL_CHIPS, 1) if down == 0 else (1, ALL_CHIPS), down)
    table = jnp.zeros(line.shape, F32)
    for j, at in enumerate(OFFSETS):
        table = jnp.where(line == at, float(j), table)
    shape = (ALL_CHIPS, offset.shape[1]) if down == 0 else (offset.shape[0], ALL_CHIPS)
    found = jnp.where(iota(shape, down) == offset, table, 0.0)
    return jnp.sum(found, axis=down, keepdims=True).astype(jnp.int32)


def message_of(device, sign):
    slide, z, y, core = where_am_i()
    by_slide = (sign * (device // 32 - slide)) & 3
    by_z = (sign * ((device // 8) % 4 - z)) & 3
    by_y = (sign * ((device // 2) % 4 - y)) & 3
    offset = by_slide * 16 + by_z * 4 + by_y
    return message_at(offset), device % 2


def own_targets(dest_ref):
    slide, z, y, core = where_am_i()
    me = slide * 32 + z * 8 + y * 2 + core
    own = jnp.concatenate([dest_ref[pl.ds(2 * me, 1), :], dest_ref[pl.ds(2 * me + 1, 1), :]], axis=1)
    device = jnp.broadcast_to(own // ROWS, (ROWS, ROWS))
    target = device.astype(F32)
    across = target.T
    same = across == target
    before_row = iota((ROWS, ROWS), 0) < iota((ROWS, ROWS), 1)
    before_col = iota((ROWS, ROWS), 1) < iota((ROWS, ROWS), 0)
    rank_row = jnp.sum(jnp.where(same & before_row, 1.0, 0.0), axis=0, keepdims=True)
    rank_col = jnp.sum(jnp.where(same & before_col, 1.0, 0.0), axis=1, keepdims=True)
    row = message_of(device[0:1, :], 1)
    col = message_of(across[:, 0:1].astype(jnp.int32), 1)
    send_row = row[0] * 8 + row[1] * SLOTS + rank_row.astype(jnp.int32)
    back_col = (col[1] ^ core) * (PACKED // 2) + col[0] * SLOTS + rank_col.astype(jnp.int32)
    return send_row, back_col


def receive_positions(dest_ref):
    slide, z, y, core = where_am_i()
    me = slide * 32 + z * 8 + y * 2 + core
    half = ROWS // 2
    dest = dest_ref[...].astype(F32).T.astype(jnp.int32)
    mine = dest // ROWS == me
    marks = onehot(mine)
    before = onehot(iota((half, half), 1) < iota((half, half), 0))
    lane = iota((ROWS, ROWS), 1)
    first_half = onehot((iota((ROWS, ROWS), 0) == lane - 1) & (lane % 2 == 1))
    count = mm(jnp.ones((half, half), BF16), marks).astype(BF16)
    rank = mm(before, marks) + mm(count, first_half)
    place = jnp.where(mine, (dest % ROWS).astype(F32) + 1.0, 0.0)
    message, sender_core = message_of(iota((ROWS, 1), 0) // 2, -1)
    slot = (sender_core ^ core) * (PACKED // 2) + message * SLOTS
    column = iota((ROWS, PACKED), 1)
    total = jnp.zeros((8, PACKED), F32)
    for k in range(SLOTS):
        held = jnp.sum(jnp.where(rank == k, place, 0.0), axis=0, keepdims=True)
        total = total + mm(jnp.broadcast_to(held, (8, ROWS)).astype(BF16), onehot(column == slot + k))
    return total - 1.0


def head_of_row():
    return iota((ROWS, D), 0) % 16 == iota((ROWS, D), 1) // 64


def normalize(hidden):
    centre = jnp.mean(hidden, axis=1, keepdims=True)
    centered = hidden - centre
    spread = jnp.mean(centered * centered, axis=1, keepdims=True)
    inverse = lax.rsqrt(spread + 1e-05)
    return centered * inverse, inverse


def block_kernel(
    tiles_hbm, dest_ref, gain_ref, w_in_hbm, wq_hbm, wk_hbm, wv_hbm, wo_hbm, og_hbm,
    layer_ref, back_ref,
    tiles_ref, w_in_ref, wq_ref, wk_ref, wv_ref, wo_ref, og_ref,
    rows_ref, out_ref, mid_ref, over_ref, out2_ref, mid2_ref, over2_ref,
    hidden_ref, q_ref, k_ref, v_ref, g_ref, far_ref,
    att_ref, dq_ref, dk_ref, dv_ref,
    qg_ref, near_ref, stat_ref, scores_ref, work_ref, keep_ref, half_send, half_recv, part_send, part_recv,
    load_sem, x_send, x_recv, o_send, o_recv,
    g_send, g_recv, f_send, f_recv, h_send, h_recv, p_send, p_recv,
):
    slide, z, y, core = where_am_i()
    chip = z * 4 + y
    other_core = 1 - core
    partner = (slide, chip * 2 + other_core)

    def ahead(r):
        return ((z + r // 4) % 4) * 4 + (y + r % 4) % 4

    def same_core(other):
        return (slide, other * 2 + core)

    def chip_rows(other):
        return pl.ds(pl.multiple_of(other * FAR, FAR), FAR)

    def at_offset(offset, sign=1):
        to_slide = (slide + 4 + sign * (offset // 16)) % 4
        to_z = (z + 4 + sign * (offset // 4 % 4)) % 4
        to_y = (y + 4 + sign * (offset % 4)) % 4
        return (to_slide, (to_z * 4 + to_y) * 2 + core)

    def loop(first, last, do):
        def step(i, carry):
            do(i)
            return carry

        lax.fori_loop(first, last, step, 0)

    loads = [
        pltpu.make_async_copy(source, target, load_sem.at[i])
        for i, (source, target) in enumerate(
            [
                (tiles_hbm, tiles_ref), (w_in_hbm, w_in_ref), (og_hbm, og_ref), (wo_hbm, wo_ref),
                (wk_hbm, wk_ref), (wv_hbm, wv_ref), (wq_hbm, wq_ref),
            ]
        )
    ]
    for load in loads[:2]:
        load.start()

    barrier = pltpu.get_barrier_semaphore()

    def greet(j):
        device = at_offset(OFFSETS[j])
        pl.semaphore_signal(barrier, inc=1, device_id=device, device_id_type=MESH)

    for j in range(1, ALL_CHIPS):
        greet(j)
    pl.semaphore_signal(barrier, inc=1, device_id=partner, device_id_type=MESH)

    def message(way, j, source, landing):
        device = at_offset(OFFSETS[j], 1 - 2 * way)
        return pltpu.make_async_remote_copy(
            src_ref=source.at[j], dst_ref=landing.at[j],
            send_sem=x_send.at[way], recv_sem=x_recv.at[way, j // GROUP],
            device_id=device, device_id_type=MESH,
        )

    def hand_over(way, group, landing, over):
        part = pl.ds(group * GROUP, GROUP)
        return pltpu.make_async_remote_copy(
            src_ref=landing.at[part, other_core], dst_ref=over.at[part],
            send_sem=o_send.at[way, group], recv_sem=o_recv.at[way, group],
            device_id=partner, device_id_type=MESH,
        )

    def exchange_start(way, source, landing, pack_step):
        for group in range(GROUPS):
            first = group * GROUP
            pack_step(first, first + GROUP)
            if way == 0 and group == 0:
                pl.semaphore_wait(barrier, ALL_CHIPS)
            for j in range(max(first, 1), first + GROUP):
                message(way, j, source, landing).start()
        landing[0] = source[0]

    def to_rows(group, first_row, chunk):
        def step(i, carry):
            rows = jnp.concatenate([chunk(2 * i).astype(F32), chunk(2 * i + 1).astype(F32)], axis=0)
            rows_ref[pl.ds(pl.multiple_of(first_row + i * 8, 8), 8), :] = rows
            return carry

        lax.fori_loop(group * GROUP // 2, (group + 1) * GROUP // 2, step, 0, unroll=8)

    def exchange_arrive(way, source, landing, over):
        for group in range(GROUPS):
            arrived = pl.ds(group * GROUP + (group == 0), GROUP - (group == 0))
            pltpu.make_async_copy(source.at[arrived], landing.at[arrived], x_recv.at[way, group]).wait()
            hand_over(way, group, landing, over).start()
            to_rows(group, 0, lambda j: landing[j, core])

    def over_rows(way, landing, over):
        for group in range(GROUPS):
            hand_over(way, group, landing, over).wait_recv()
            to_rows(group, PACKED // 2, lambda j: over[j])

    def exchange_sent(way, source, landing, over):
        left = pl.ds(1, ALL_CHIPS - 1)
        pltpu.make_async_copy(source.at[left], landing.at[left], x_send.at[way]).wait()
        for group in range(GROUPS):
            hand_over(way, group, landing, over).wait_send()

    send_row, back_col = own_targets(dest_ref)
    pack = onehot(iota((PACKED, ROWS), 0) == send_row)
    pick_back = onehot(iota((ROWS, PACKED), 1) == back_col)
    loads[0].wait()
    loads[1].wait()
    for load in loads[2:]:
        load.start()
    rows_ref[...] = mm(pack, mm(tiles_ref[...], w_in_ref[...]).astype(BF16))

    def pack_send(first, last):
        def step(j, carry):
            rows = rows_ref[pl.ds(pl.multiple_of(j * 8, 8), 8), :].astype(BF16)
            out_ref[j, 0] = rows[0:4]
            out_ref[j, 1] = rows[4:8]
            return carry

        lax.fori_loop(first, last, step, 0, unroll=8)

    exchange_start(0, out_ref, mid_ref, pack_send)

    position = receive_positions(dest_ref)
    place = onehot(iota((ROWS, PACKED), 0).astype(F32) == position[0:1, :])
    loads[2].wait()
    loads[3].wait()
    g_ref[...] = mm_nt(og_ref[...], wo_ref[...]).astype(BF16)
    loads[4].wait()
    loads[5].wait()
    loads[6].wait()

    exchange_arrive(0, out_ref, mid_ref, over_ref)
    hidden = mm(place[:, : PACKED // 2], rows_ref[: PACKED // 2].astype(BF16))
    over_rows(0, mid_ref, over_ref)
    hidden = hidden + mm(place[:, PACKED // 2 :], rows_ref[PACKED // 2 :].astype(BF16))
    hidden_ref[...] = hidden.astype(BF16)
    normalized, _ = normalize(hidden)
    gain = gain_ref[...].reshape(1, D)
    normed = (normalized * gain).astype(BF16)
    k_ref[...] = mm(normed, wk_ref[...]).astype(BF16)
    v_ref[...] = mm(normed, wv_ref[...]).astype(BF16)

    chosen = head_of_row()
    pick = onehot(iota((FAR, ROWS), 0) == iota((FAR, ROWS), 1) // 16)
    none = jnp.zeros((ROWS, D), BF16)
    own = chip_rows(chip)
    far_k = mm(pick, jnp.where(chosen, k_ref[...], none)).astype(BF16)
    far_v = mm(pick, jnp.where(chosen, v_ref[...], none)).astype(BF16)
    for c in range(PAIRS):
        far_ref[c, 0, own, 0:LANES] = far_k[:, c * LANES : (c + 1) * LANES]
        far_ref[c, 0, own, LANES:] = far_v[:, c * LANES : (c + 1) * LANES]

    def gather_copy(c, r):
        return pltpu.make_async_remote_copy(
            src_ref=far_ref.at[c, 0, own], dst_ref=far_ref.at[c, 0, own],
            send_sem=g_send.at[c], recv_sem=g_recv.at[c],
            device_id=same_core(ahead(r)), device_id_type=MESH,
        )

    def forward_copy(c):
        return pltpu.make_async_remote_copy(
            src_ref=far_ref.at[c, 0], dst_ref=far_ref.at[c, 1],
            send_sem=f_send.at[c], recv_sem=f_recv.at[c],
            device_id=partner, device_id_type=MESH,
        )

    def pass_on(c):
        fifteen = far_ref.at[c, 0, pl.ds(0, HALF - FAR)]
        pltpu.make_async_copy(fifteen, fifteen, g_recv.at[c]).wait()
        forward_copy(c).start()

    def gather_start(c):
        for r in FAR_FIRST:
            gather_copy(c, r).start()

    loop(0, PAIRS, gather_start)
    q_ref[...] = mm(normed, wq_ref[...]).astype(BF16) * jnp.bfloat16(0.125)

    low = iota((ROWS, LANES), 1) < 64
    zero = jnp.zeros((ROWS, LANES), BF16)
    wide = 2 * ROWS

    def near(c):
        cols = pl.ds(pl.multiple_of(c * LANES, LANES), LANES)
        for first, pair in ((0, q_ref[:, cols]), (wide, g_ref[:, cols])):
            qg_ref[c, first : first + ROWS] = jnp.where(low, pair, zero)
            qg_ref[c, first + ROWS : first + wide] = jnp.where(low, zero, pair)
        near_ref[c, :, :wide] = mm_nt(k_ref[:, cols], qg_ref[c, :wide])
        near_ref[c, :, wide:] = mm_nt(v_ref[:, cols], qg_ref[c, wide:])
        top, total, inner = grow(near_ref.at[c], ROWS)
        stat_ref[c, 0:1] = top
        stat_ref[c, 1:2] = total
        stat_ref[c, 2:3] = inner

    def grow(matrix, count):
        strips = [slice(i, i + STRIP) for i in range(0, count, STRIP)]
        top = matrix[strips[0], :wide]
        for strip in strips[1:]:
            top = jnp.maximum(top, matrix[strip, :wide])
        top = jnp.max(top, axis=0, keepdims=True)
        total = jnp.zeros((STRIP, wide), F32)
        inner = jnp.zeros((STRIP, wide), F32)
        for strip in strips:
            grown = jnp.exp(matrix[strip, :wide] - top)
            matrix[strip, :wide] = grown
            total = total + grown
            inner = inner + grown * matrix[strip, wide:]
        return top, jnp.sum(total, axis=0, keepdims=True), jnp.sum(inner, axis=0, keepdims=True)

    def shrink(c, matrix, first, count, factor, delta):
        for i in range(0, count, STRIP):
            prob = matrix[i : i + STRIP, :wide] * factor
            out = slice(first + i, first + i + STRIP)
            work_ref[c, out, :wide] = (prob * (matrix[i : i + STRIP, wide:] - delta)).astype(BF16)
            work_ref[c, out, wide:] = prob.astype(BF16)

    loop(0, PAIRS, near)
    pass_on(0)

    def half_copy(c):
        return pltpu.make_async_remote_copy(
            src_ref=half_send.at[c], dst_ref=half_recv.at[c],
            send_sem=h_send.at[c], recv_sem=h_recv.at[c],
            device_id=partner, device_id_type=MESH,
        )

    def part_copy(c, r):
        other = ahead(r)
        return pltpu.make_async_remote_copy(
            src_ref=part_send.at[c, chip_rows(other)], dst_ref=part_recv.at[c, own],
            send_sem=p_send.at[c], recv_sem=p_recv.at[c],
            device_id=same_core(other), device_id_type=MESH,
        )

    def share(c):
        half_copy(c).wait_recv()
        part_send[c] = (keep_ref[c] + half_recv[c].astype(F32)).astype(BF16)
        part_recv[c, own] = part_send[c, own]
        for r in FAR_FIRST:
            part_copy(c, r).start()

    def mixed(near_t, far_t, near_w, far_w):
        first = mm(near_t[:64], near_w[:, :ROWS]) + mm(far_t[:64], far_w[:, :ROWS])
        second = mm(near_t[64:], near_w[:, ROWS:]) + mm(far_t[64:], far_w[:, ROWS:])
        return jnp.concatenate([first, second], axis=0).T

    def attend(c):
        forward_copy(c).wait_recv()

        @pl.when(c < PAIRS - 1)
        def _():
            pass_on(c + 1)

        q2, g2 = qg_ref[c, :wide], qg_ref[c, wide:]
        scores_ref[:, :wide] = mm_nt(far_ref[c, :, :, 0:LANES].reshape(2 * HALF, LANES), q2)
        scores_ref[:, wide:] = mm_nt(far_ref[c, :, :, LANES:].reshape(2 * HALF, LANES), g2)
        top, total, inner = grow(scores_ref, 2 * HALF)
        near_top = stat_ref[c, 0:1]
        joint = jnp.maximum(top, near_top)
        near_part, far_part = jnp.exp(near_top - joint), jnp.exp(top - joint)
        inv = 1.0 / (near_part * stat_ref[c, 1:2] + far_part * total)
        delta = (near_part * stat_ref[c, 2:3] + far_part * inner) * inv
        stat_ref[c, 3:4] = near_part * inv
        stat_ref[c, 4:5] = delta
        shrink(c, scores_ref, ROWS, 2 * HALF, far_part * inv, delta)
        far_k_sum = mm(work_ref[c, ROWS:, :wide], q2)
        far_v_sum = mm(work_ref[c, ROWS:, wide:], g2)
        keep_ref[c, :, :LANES] = far_k_sum[:HALF]
        keep_ref[c, :, LANES:] = far_v_sum[:HALF]
        half_send[c, :, :LANES] = far_k_sum[HALF:].astype(BF16)
        half_send[c, :, LANES:] = far_v_sum[HALF:].astype(BF16)
        half_copy(c).start()

        @pl.when(c > 0)
        def _():
            share(c - 1)

    def gather_up(c):
        cols = pl.ds(pl.multiple_of(c * LANES, LANES), LANES)
        shrink(c, near_ref.at[c], 0, ROWS, stat_ref[c, 3:4], stat_ref[c, 4:5])
        dk_ref[:, cols] = mm(work_ref[c, :ROWS, :wide], qg_ref[c, :wide])
        dv_ref[:, cols] = mm(work_ref[c, :ROWS, wide:], qg_ref[c, wide:])
        kf = far_ref[c, :, :, 0:LANES].reshape(2 * HALF, LANES)
        vf = far_ref[c, :, :, LANES:].reshape(2 * HALF, LANES)
        weights, slopes = work_ref[c, :, wide:], work_ref[c, :, :wide]
        att_ref[:, cols] = mixed(v_ref[:, cols].T, vf.T, weights[:ROWS], weights[ROWS:]).astype(BF16)
        dq_ref[:, cols] = (mixed(k_ref[:, cols].T, kf.T, slopes[:ROWS], slopes[ROWS:]) * 0.125).astype(BF16)

        @pl.when(c == 0)
        def _():
            share(PAIRS - 1)

    loop(0, PAIRS, attend)
    loop(0, PAIRS, gather_up)

    hidden = hidden_ref[...].astype(F32)
    grad_normed = mm_nt(dq_ref[...], wq_ref[...])
    layer_ref[...] = (hidden + mm(att_ref[...], wo_ref[...])).astype(BF16)
    column = position.T[:, 0:1]
    unplace = onehot(iota((PACKED, ROWS), 1).astype(F32) == column)

    def add_far(c, carry):
        fifteen = pl.ds(0, HALF - FAR)
        pltpu.make_async_copy(part_send.at[c, fifteen], part_recv.at[c, fifteen], p_recv.at[c]).wait()
        cols = pl.ds(pl.multiple_of(c * LANES, LANES), LANES)
        total = jnp.sum(part_recv[c].astype(F32).reshape(CHIPS, FAR, 2 * LANES), axis=0)
        spread = jnp.broadcast_to(total[:, None, :], (FAR, 16, 2 * LANES)).reshape(ROWS, 2 * LANES)
        seen = iota((ROWS, LANES), 0) % 16 == iota((ROWS, LANES), 1) // 64 + 2 * c
        dk_ref[:, cols] += jnp.where(seen, spread[:, :LANES], 0.0)
        dv_ref[:, cols] += jnp.where(seen, spread[:, LANES:], 0.0)
        return carry

    def project_back(cols):
        grads = jnp.concatenate([dk_ref[:, cols], dv_ref[:, cols]], axis=1).astype(BF16)
        return mm_nt(grads, jnp.concatenate([wk_ref[:, cols], wv_ref[:, cols]], axis=1))

    early = PAIRS - 2
    lax.fori_loop(0, early, add_far, 0)
    grad_normed = grad_normed + project_back(slice(0, early * LANES))
    lax.fori_loop(early, PAIRS, add_far, 0)
    grad_normed = grad_normed + project_back(slice(early * LANES, D))
    normalized, inverse = normalize(hidden)
    scaled = grad_normed * gain
    inner = (
        scaled
        - jnp.mean(scaled, axis=1, keepdims=True)
        - normalized * jnp.mean(scaled * normalized, axis=1, keepdims=True)
    )
    grad_hidden = (og_ref[...].astype(F32) + inner * inverse).astype(BF16)

    rows_ref[...] = mm(unplace, grad_hidden)

    def pack_back(first, last):
        def step(i, carry):
            mine = rows_ref[pl.ds(pl.multiple_of(i * 8, 8), 8), :].astype(BF16)
            theirs = rows_ref[pl.ds(pl.multiple_of(PACKED // 2 + i * 8, 8), 8), :].astype(BF16)
            out2_ref[2 * i, core] = mine[0:4]
            out2_ref[2 * i + 1, core] = mine[4:8]
            out2_ref[2 * i, other_core] = theirs[0:4]
            out2_ref[2 * i + 1, other_core] = theirs[4:8]
            return carry

        lax.fori_loop(first // 2, last // 2, step, 0, unroll=8)

    exchange_start(1, out2_ref, mid2_ref, pack_back)

    exchange_sent(0, out_ref, mid_ref, over_ref)

    def sent(c):
        fifteen = far_ref.at[c, 0, pl.ds(0, HALF - FAR)]
        pltpu.make_async_copy(fifteen, fifteen, g_send.at[c]).wait()
        forward_copy(c).wait_send()
        half_copy(c).wait_send()
        parts = part_send.at[c, pl.ds(0, HALF - FAR)]
        pltpu.make_async_copy(parts, parts, p_send.at[c]).wait()

    loop(0, PAIRS, sent)

    exchange_arrive(1, out2_ref, mid2_ref, over2_ref)
    back = mm(pick_back[:, : PACKED // 2], rows_ref[: PACKED // 2].astype(BF16))
    over_rows(1, mid2_ref, over2_ref)
    back = back + mm(pick_back[:, PACKED // 2 :], rows_ref[PACKED // 2 :].astype(BF16))
    back_ref[...] = back.astype(BF16)
    exchange_sent(1, out2_ref, mid2_ref, over2_ref)


def per_device(tiles, dest_row, w_in, norm_gain, w_query, w_key, w_value, w_out, out_grad):
    vmem = pl.BlockSpec(memory_space=pltpu.VMEM)
    hbm = pl.BlockSpec(memory_space=pl.ANY)
    dma = pltpu.SemaphoreType.DMA
    slots = (ALL_CHIPS, 2, SLOTS, D)
    over = (ALL_CHIPS, SLOTS, D)
    pairs = (PAIRS, HALF, 2 * LANES)

    def bf16(*shape):
        return pltpu.VMEM(shape, BF16)

    def f32(*shape):
        return pltpu.VMEM(shape, F32)

    layer, grad_hidden = pl.pallas_call(
        block_kernel,
        out_shape=(jax.ShapeDtypeStruct((ROWS, D), BF16), jax.ShapeDtypeStruct((ROWS, D), BF16)),
        in_specs=[hbm, vmem, vmem] + [hbm] * 6,
        out_specs=(vmem, vmem),
        scratch_shapes=[
            bf16(ROWS, WIDTH), bf16(WIDTH, D), bf16(D, D), bf16(D, D), bf16(D, D), bf16(D, D), bf16(ROWS, D),
            f32(PACKED, D), bf16(*slots), bf16(*slots), bf16(*over), bf16(*slots), bf16(*slots), bf16(*over),
            bf16(ROWS, D), bf16(ROWS, D), bf16(ROWS, D), bf16(ROWS, D), bf16(ROWS, D),
            bf16(PAIRS, 2, HALF, 2 * LANES),
            bf16(ROWS, D), bf16(ROWS, D), f32(ROWS, D), f32(ROWS, D),
            bf16(PAIRS, 4 * ROWS, LANES), f32(PAIRS, ROWS, 4 * ROWS), f32(PAIRS, 8, 2 * ROWS),
            f32(2 * HALF, 4 * ROWS), bf16(PAIRS, ROWS + 2 * HALF, 4 * ROWS),
            f32(*pairs), bf16(*pairs), bf16(*pairs), bf16(*pairs), bf16(*pairs),
            dma((7,)), dma((2,)), dma((2, GROUPS)), dma((2, GROUPS)), dma((2, GROUPS)),
            dma((PAIRS,)), dma((PAIRS,)), dma((PAIRS,)), dma((PAIRS,)),
            dma((PAIRS,)), dma((PAIRS,)), dma((PAIRS,)), dma((PAIRS,)),
        ],
        compiler_params=pltpu.CompilerParams(
            vmem_limit_bytes=VMEM_LIMIT, collective_id=0, has_side_effects=True
        ),
    )(tiles, dest_row.reshape(ROWS, DEVICES), norm_gain, w_in, w_query, w_key, w_value, w_out, out_grad)
    return layer, mm_nt(grad_hidden, w_in).astype(BF16)


def solution(mesh):
    split = P(("slide", "seq"), None)
    return jax.shard_map(
        per_device,
        mesh=mesh,
        in_specs=(split, P(), P(), P(), P(), P(), P(), P(), split),
        out_specs=(split, split),
        check_vma=False,
    )
```

```python
import jax
import jax.numpy as jnp
from jax import lax
from jax.experimental import pallas as pl
from jax.experimental.pallas import tpu as pltpu
from jax.sharding import PartitionSpec as P

ROWS = 256
WIDTH = 1536
D = 768
DEVICES = 128
SLOTS = 4
PACKED = DEVICES * SLOTS
ALL_CHIPS = 64
GROUPS = 4
GROUP = ALL_CHIPS // GROUPS
CHIPS = 16
FAR_FIRST = (10, 9, 11, 6, 14, 2, 8, 5, 7, 13, 15, 1, 3, 4, 12)
FAR = 16
HALF = CHIPS * FAR
PAIRS = 6
STRIP = 16
LANES = 128
MESH = pl.DeviceIdType.MESH


def hops(offset):
    return sum(min(part, 4 - part) for part in (offset // 16, offset // 4 % 4, offset % 4))


OFFSETS = [0] + sorted(range(1, ALL_CHIPS), key=lambda o: (-hops(o), o * 45 % 64))
F32 = jnp.float32
BF16 = jnp.bfloat16
VMEM_LIMIT = 60 * 1024 * 1024


def mm(left, right):
    return jnp.dot(left, right, preferred_element_type=F32)


def mm_nt(left, right):
    return lax.dot_general(left, right, (((1,), (1,)), ((), ())), preferred_element_type=F32)


def iota(shape, dim):
    return lax.broadcasted_iota(jnp.int32, shape, dim)


def onehot(cond):
    return jnp.where(cond, 1.0, 0.0).astype(BF16)


def where_am_i():
    slide, seq = lax.axis_index("slide"), lax.axis_index("seq")
    return slide, seq // 8, (seq // 2) % 4, seq % 2


def message_at(offset):
    down = 0 if offset.shape[0] == 1 else 1
    line = iota((ALL_CHIPS, 1) if down == 0 else (1, ALL_CHIPS), down)
    table = jnp.zeros(line.shape, F32)
    for j, at in enumerate(OFFSETS):
        table = jnp.where(line == at, float(j), table)
    shape = (ALL_CHIPS, offset.shape[1]) if down == 0 else (offset.shape[0], ALL_CHIPS)
    found = jnp.where(iota(shape, down) == offset, table, 0.0)
    return jnp.sum(found, axis=down, keepdims=True).astype(jnp.int32)


def message_of(device, sign):
    slide, z, y, core = where_am_i()
    by_slide = (sign * (device // 32 - slide)) & 3
    by_z = (sign * ((device // 8) % 4 - z)) & 3
    by_y = (sign * ((device // 2) % 4 - y)) & 3
    offset = by_slide * 16 + by_z * 4 + by_y
    return message_at(offset), device % 2


def own_targets(dest_ref):
    slide, z, y, core = where_am_i()
    me = slide * 32 + z * 8 + y * 2 + core
    own = jnp.concatenate([dest_ref[pl.ds(2 * me, 1), :], dest_ref[pl.ds(2 * me + 1, 1), :]], axis=1)
    device = jnp.broadcast_to(own // ROWS, (ROWS, ROWS))
    target = device.astype(F32)
    across = target.T
    same = across == target
    before_row = iota((ROWS, ROWS), 0) < iota((ROWS, ROWS), 1)
    before_col = iota((ROWS, ROWS), 1) < iota((ROWS, ROWS), 0)
    rank_row = jnp.sum(jnp.where(same & before_row, 1.0, 0.0), axis=0, keepdims=True)
    rank_col = jnp.sum(jnp.where(same & before_col, 1.0, 0.0), axis=1, keepdims=True)
    row = message_of(device[0:1, :], 1)
    col = message_of(across[:, 0:1].astype(jnp.int32), 1)
    send_row = row[0] * 8 + row[1] * SLOTS + rank_row.astype(jnp.int32)
    back_col = (col[1] ^ core) * (PACKED // 2) + col[0] * SLOTS + rank_col.astype(jnp.int32)
    return send_row, back_col


def receive_positions(dest_ref):
    slide, z, y, core = where_am_i()
    me = slide * 32 + z * 8 + y * 2 + core
    half = ROWS // 2
    dest = dest_ref[...].astype(F32).T.astype(jnp.int32)
    mine = dest // ROWS == me
    marks = onehot(mine)
    before = onehot(iota((half, half), 1) < iota((half, half), 0))
    lane = iota((ROWS, ROWS), 1)
    first_half = onehot((iota((ROWS, ROWS), 0) == lane - 1) & (lane % 2 == 1))
    count = mm(jnp.ones((half, half), BF16), marks).astype(BF16)
    rank = mm(before, marks) + mm(count, first_half)
    place = jnp.where(mine, (dest % ROWS).astype(F32) + 1.0, 0.0)
    message, sender_core = message_of(iota((ROWS, 1), 0) // 2, -1)
    slot = (sender_core ^ core) * (PACKED // 2) + message * SLOTS
    column = iota((ROWS, PACKED), 1)
    total = jnp.zeros((8, PACKED), F32)
    for k in range(SLOTS):
        held = jnp.sum(jnp.where(rank == k, place, 0.0), axis=0, keepdims=True)
        total = total + mm(jnp.broadcast_to(held, (8, ROWS)).astype(BF16), onehot(column == slot + k))
    return total - 1.0


def head_of_row():
    return iota((ROWS, D), 0) % 16 == iota((ROWS, D), 1) // 64


def normalize(hidden):
    centre = jnp.mean(hidden, axis=1, keepdims=True)
    centered = hidden - centre
    spread = jnp.mean(centered * centered, axis=1, keepdims=True)
    inverse = lax.rsqrt(spread + 1e-05)
    return centered * inverse, inverse


def block_kernel(
    tiles_hbm, dest_ref, gain_ref, w_in_hbm, wq_hbm, wk_hbm, wv_hbm, wo_hbm, og_hbm,
    layer_ref, back_ref,
    tiles_ref, w_in_ref, wq_ref, wk_ref, wv_ref, wo_ref, og_ref,
    rows_ref, out_ref, mid_ref, over_ref, out2_ref, mid2_ref, over2_ref,
    hidden_ref, q_ref, k_ref, v_ref, g_ref, far_ref,
    att_ref, dq_ref, dk_ref, dv_ref,
    qg_ref, near_ref, stat_ref, scores_ref, work_ref, keep_ref, half_send, half_recv, part_send, part_recv,
    load_sem, x_send, x_recv, o_send, o_recv,
    g_send, g_recv, f_send, f_recv, h_send, h_recv, p_send, p_recv,
):
    slide, z, y, core = where_am_i()
    chip = z * 4 + y
    other_core = 1 - core
    partner = (slide, chip * 2 + other_core)

    def ahead(r):
        return ((z + r // 4) % 4) * 4 + (y + r % 4) % 4

    def same_core(other):
        return (slide, other * 2 + core)

    def chip_rows(other):
        return pl.ds(pl.multiple_of(other * FAR, FAR), FAR)

    def at_offset(offset, sign=1):
        to_slide = (slide + 4 + sign * (offset // 16)) % 4
        to_z = (z + 4 + sign * (offset // 4 % 4)) % 4
        to_y = (y + 4 + sign * (offset % 4)) % 4
        return (to_slide, (to_z * 4 + to_y) * 2 + core)

    def loop(first, last, do):
        def step(i, carry):
            do(i)
            return carry

        lax.fori_loop(first, last, step, 0)

    loads = [
        pltpu.make_async_copy(source, target, load_sem.at[i])
        for i, (source, target) in enumerate(
            [
                (tiles_hbm, tiles_ref), (w_in_hbm, w_in_ref), (og_hbm, og_ref), (wo_hbm, wo_ref),
                (wk_hbm, wk_ref), (wv_hbm, wv_ref), (wq_hbm, wq_ref),
            ]
        )
    ]
    for load in loads[:2]:
        load.start()

    barrier = pltpu.get_barrier_semaphore()

    def greet(j):
        device = at_offset(OFFSETS[j])
        pl.semaphore_signal(barrier, inc=1, device_id=device, device_id_type=MESH)

    for j in range(1, ALL_CHIPS):
        greet(j)
    pl.semaphore_signal(barrier, inc=1, device_id=partner, device_id_type=MESH)

    def message(way, j, source, landing):
        device = at_offset(OFFSETS[j], 1 - 2 * way)
        return pltpu.make_async_remote_copy(
            src_ref=source.at[j], dst_ref=landing.at[j],
            send_sem=x_send.at[way], recv_sem=x_recv.at[way, j // GROUP],
            device_id=device, device_id_type=MESH,
        )

    def hand_over(way, group, landing, over):
        part = pl.ds(group * GROUP, GROUP)
        return pltpu.make_async_remote_copy(
            src_ref=landing.at[part, other_core], dst_ref=over.at[part],
            send_sem=o_send.at[way, group], recv_sem=o_recv.at[way, group],
            device_id=partner, device_id_type=MESH,
        )

    def exchange_start(way, source, landing, pack_step):
        for group in range(GROUPS):
            first = group * GROUP
            pack_step(first, first + GROUP)
            if way == 0 and group == 0:
                pl.semaphore_wait(barrier, ALL_CHIPS)
            for j in range(max(first, 1), first + GROUP):
                message(way, j, source, landing).start()
        landing[0] = source[0]

    def to_rows(group, first_row, chunk):
        def step(i, carry):
            rows = jnp.concatenate([chunk(2 * i).astype(F32), chunk(2 * i + 1).astype(F32)], axis=0)
            rows_ref[pl.ds(pl.multiple_of(first_row + i * 8, 8), 8), :] = rows
            return carry

        lax.fori_loop(group * GROUP // 2, (group + 1) * GROUP // 2, step, 0, unroll=8)

    def exchange_arrive(way, source, landing, over):
        for group in range(GROUPS):
            arrived = pl.ds(group * GROUP + (group == 0), GROUP - (group == 0))
            pltpu.make_async_copy(source.at[arrived], landing.at[arrived], x_recv.at[way, group]).wait()
            hand_over(way, group, landing, over).start()
            to_rows(group, 0, lambda j: landing[j, core])

    def over_rows(way, landing, over):
        for group in range(GROUPS):
            hand_over(way, group, landing, over).wait_recv()
            to_rows(group, PACKED // 2, lambda j: over[j])

    def exchange_sent(way, source, landing, over):
        left = pl.ds(1, ALL_CHIPS - 1)
        pltpu.make_async_copy(source.at[left], landing.at[left], x_send.at[way]).wait()
        for group in range(GROUPS):
            hand_over(way, group, landing, over).wait_send()

    send_row, back_col = own_targets(dest_ref)
    pack = onehot(iota((PACKED, ROWS), 0) == send_row)
    pick_back = onehot(iota((ROWS, PACKED), 1) == back_col)
    loads[0].wait()
    loads[1].wait()
    for load in loads[2:]:
        load.start()
    rows_ref[...] = mm(pack, mm(tiles_ref[...], w_in_ref[...]).astype(BF16))

    def pack_send(first, last):
        def step(j, carry):
            rows = rows_ref[pl.ds(pl.multiple_of(j * 8, 8), 8), :].astype(BF16)
            out_ref[j, 0] = rows[0:4]
            out_ref[j, 1] = rows[4:8]
            return carry

        lax.fori_loop(first, last, step, 0, unroll=8)

    exchange_start(0, out_ref, mid_ref, pack_send)

    position = receive_positions(dest_ref)
    place = onehot(iota((ROWS, PACKED), 0).astype(F32) == position[0:1, :])
    loads[2].wait()
    loads[3].wait()
    g_ref[...] = mm_nt(og_ref[...], wo_ref[...]).astype(BF16)
    loads[4].wait()
    loads[5].wait()
    loads[6].wait()

    exchange_arrive(0, out_ref, mid_ref, over_ref)
    hidden = mm(place[:, : PACKED // 2], rows_ref[: PACKED // 2].astype(BF16))
    over_rows(0, mid_ref, over_ref)
    hidden = hidden + mm(place[:, PACKED // 2 :], rows_ref[PACKED // 2 :].astype(BF16))
    hidden_ref[...] = hidden.astype(BF16)
    normalized, _ = normalize(hidden)
    gain = gain_ref[...].reshape(1, D)
    normed = (normalized * gain).astype(BF16)
    k_ref[...] = mm(normed, wk_ref[...]).astype(BF16)
    v_ref[...] = mm(normed, wv_ref[...]).astype(BF16)

    chosen = head_of_row()
    pick = onehot(iota((FAR, ROWS), 0) == iota((FAR, ROWS), 1) // 16)
    none = jnp.zeros((ROWS, D), BF16)
    own = chip_rows(chip)
    far_k = mm(pick, jnp.where(chosen, k_ref[...], none)).astype(BF16)
    far_v = mm(pick, jnp.where(chosen, v_ref[...], none)).astype(BF16)
    for c in range(PAIRS):
        far_ref[c, 0, own, 0:LANES] = far_k[:, c * LANES : (c + 1) * LANES]
        far_ref[c, 0, own, LANES:] = far_v[:, c * LANES : (c + 1) * LANES]

    def gather_copy(c, r):
        return pltpu.make_async_remote_copy(
            src_ref=far_ref.at[c, 0, own], dst_ref=far_ref.at[c, 0, own],
            send_sem=g_send.at[c], recv_sem=g_recv.at[c],
            device_id=same_core(ahead(r)), device_id_type=MESH,
        )

    def forward_copy(c):
        return pltpu.make_async_remote_copy(
            src_ref=far_ref.at[c, 0], dst_ref=far_ref.at[c, 1],
            send_sem=f_send.at[c], recv_sem=f_recv.at[c],
            device_id=partner, device_id_type=MESH,
        )

    def pass_on(c):
        fifteen = far_ref.at[c, 0, pl.ds(0, HALF - FAR)]
        pltpu.make_async_copy(fifteen, fifteen, g_recv.at[c]).wait()
        forward_copy(c).start()

    def gather_start(c):
        for r in FAR_FIRST:
            gather_copy(c, r).start()

    loop(0, PAIRS, gather_start)
    q_ref[...] = mm(normed, wq_ref[...]).astype(BF16) * jnp.bfloat16(0.125)

    low = iota((ROWS, LANES), 1) < 64
    zero = jnp.zeros((ROWS, LANES), BF16)
    wide = 2 * ROWS

    def near(c):
        cols = pl.ds(pl.multiple_of(c * LANES, LANES), LANES)
        for first, pair in ((0, q_ref[:, cols]), (wide, g_ref[:, cols])):
            qg_ref[c, first : first + ROWS] = jnp.where(low, pair, zero)
            qg_ref[c, first + ROWS : first + wide] = jnp.where(low, zero, pair)
        near_ref[c, :, :wide] = mm_nt(k_ref[:, cols], qg_ref[c, :wide])
        near_ref[c, :, wide:] = mm_nt(v_ref[:, cols], qg_ref[c, wide:])
        top, total, inner = grow(near_ref.at[c], ROWS)
        stat_ref[c, 0:1] = top
        stat_ref[c, 1:2] = total
        stat_ref[c, 2:3] = inner

    def grow(matrix, count):
        strips = [slice(i, i + STRIP) for i in range(0, count, STRIP)]
        top = matrix[strips[0], :wide]
        for strip in strips[1:]:
            top = jnp.maximum(top, matrix[strip, :wide])
        top = jnp.max(top, axis=0, keepdims=True)
        total = jnp.zeros((STRIP, wide), F32)
        inner = jnp.zeros((STRIP, wide), F32)
        for strip in strips:
            grown = jnp.exp(matrix[strip, :wide] - top)
            matrix[strip, :wide] = grown
            total = total + grown
            inner = inner + grown * matrix[strip, wide:]
        return top, jnp.sum(total, axis=0, keepdims=True), jnp.sum(inner, axis=0, keepdims=True)

    def shrink(c, matrix, first, count, factor, delta):
        for i in range(0, count, STRIP):
            prob = matrix[i : i + STRIP, :wide] * factor
            out = slice(first + i, first + i + STRIP)
            work_ref[c, out, :wide] = (prob * (matrix[i : i + STRIP, wide:] - delta)).astype(BF16)
            work_ref[c, out, wide:] = prob.astype(BF16)

    loop(0, PAIRS, near)
    pass_on(0)

    def half_copy(c):
        return pltpu.make_async_remote_copy(
            src_ref=half_send.at[c], dst_ref=half_recv.at[c],
            send_sem=h_send.at[c], recv_sem=h_recv.at[c],
            device_id=partner, device_id_type=MESH,
        )

    def part_copy(c, r):
        other = ahead(r)
        return pltpu.make_async_remote_copy(
            src_ref=part_send.at[c, chip_rows(other)], dst_ref=part_recv.at[c, own],
            send_sem=p_send.at[c], recv_sem=p_recv.at[c],
            device_id=same_core(other), device_id_type=MESH,
        )

    def share(c):
        half_copy(c).wait_recv()
        part_send[c] = (keep_ref[c] + half_recv[c].astype(F32)).astype(BF16)
        part_recv[c, own] = part_send[c, own]
        for r in FAR_FIRST:
            part_copy(c, r).start()

    def mixed(near_t, far_t, near_w, far_w):
        first = mm(near_t[:64], near_w[:, :ROWS]) + mm(far_t[:64], far_w[:, :ROWS])
        second = mm(near_t[64:], near_w[:, ROWS:]) + mm(far_t[64:], far_w[:, ROWS:])
        return jnp.concatenate([first, second], axis=0).T

    def attend(c):
        forward_copy(c).wait_recv()

        @pl.when(c < PAIRS - 1)
        def _():
            pass_on(c + 1)

        q2, g2 = qg_ref[c, :wide], qg_ref[c, wide:]
        scores_ref[:, :wide] = mm_nt(far_ref[c, :, :, 0:LANES].reshape(2 * HALF, LANES), q2)
        scores_ref[:, wide:] = mm_nt(far_ref[c, :, :, LANES:].reshape(2 * HALF, LANES), g2)
        top, total, inner = grow(scores_ref, 2 * HALF)
        near_top = stat_ref[c, 0:1]
        joint = jnp.maximum(top, near_top)
        near_part, far_part = jnp.exp(near_top - joint), jnp.exp(top - joint)
        inv = 1.0 / (near_part * stat_ref[c, 1:2] + far_part * total)
        delta = (near_part * stat_ref[c, 2:3] + far_part * inner) * inv
        stat_ref[c, 3:4] = near_part * inv
        stat_ref[c, 4:5] = delta
        shrink(c, scores_ref, ROWS, 2 * HALF, far_part * inv, delta)
        far_k_sum = mm(work_ref[c, ROWS:, :wide], q2)
        far_v_sum = mm(work_ref[c, ROWS:, wide:], g2)
        keep_ref[c, :, :LANES] = far_k_sum[:HALF]
        keep_ref[c, :, LANES:] = far_v_sum[:HALF]
        half_send[c, :, :LANES] = far_k_sum[HALF:].astype(BF16)
        half_send[c, :, LANES:] = far_v_sum[HALF:].astype(BF16)
        half_copy(c).start()

        @pl.when(c > 0)
        def _():
            share(c - 1)

    def gather_up(c):
        cols = pl.ds(pl.multiple_of(c * LANES, LANES), LANES)
        shrink(c, near_ref.at[c], 0, ROWS, stat_ref[c, 3:4], stat_ref[c, 4:5])
        dk_ref[:, cols] = mm(work_ref[c, :ROWS, :wide], qg_ref[c, :wide])
        dv_ref[:, cols] = mm(work_ref[c, :ROWS, wide:], qg_ref[c, wide:])
        kf = far_ref[c, :, :, 0:LANES].reshape(2 * HALF, LANES)
        vf = far_ref[c, :, :, LANES:].reshape(2 * HALF, LANES)
        weights, slopes = work_ref[c, :, wide:], work_ref[c, :, :wide]
        att_ref[:, cols] = mixed(v_ref[:, cols].T, vf.T, weights[:ROWS], weights[ROWS:]).astype(BF16)
        dq_ref[:, cols] = (mixed(k_ref[:, cols].T, kf.T, slopes[:ROWS], slopes[ROWS:]) * 0.125).astype(BF16)

        @pl.when(c == 0)
        def _():
            share(PAIRS - 1)

    loop(0, PAIRS, attend)
    loop(0, PAIRS, gather_up)

    hidden = hidden_ref[...].astype(F32)
    grad_normed = mm_nt(dq_ref[...], wq_ref[...])
    column = position.T[:, 0:1]
    unplace = onehot(iota((PACKED, ROWS), 1).astype(F32) == column)

    def add_far(c, carry):
        fifteen = pl.ds(0, HALF - FAR)
        pltpu.make_async_copy(part_send.at[c, fifteen], part_recv.at[c, fifteen], p_recv.at[c]).wait()
        cols = pl.ds(pl.multiple_of(c * LANES, LANES), LANES)
        total = jnp.sum(part_recv[c].astype(F32).reshape(CHIPS, FAR, 2 * LANES), axis=0)
        spread = jnp.broadcast_to(total[:, None, :], (FAR, 16, 2 * LANES)).reshape(ROWS, 2 * LANES)
        seen = iota((ROWS, LANES), 0) % 16 == iota((ROWS, LANES), 1) // 64 + 2 * c
        dk_ref[:, cols] += jnp.where(seen, spread[:, :LANES], 0.0)
        dv_ref[:, cols] += jnp.where(seen, spread[:, LANES:], 0.0)
        return carry

    def project_back(cols):
        grads = jnp.concatenate([dk_ref[:, cols], dv_ref[:, cols]], axis=1).astype(BF16)
        return mm_nt(grads, jnp.concatenate([wk_ref[:, cols], wv_ref[:, cols]], axis=1))

    early = PAIRS - 1
    lax.fori_loop(0, early, add_far, 0)
    grad_normed = grad_normed + project_back(slice(0, early * LANES))
    lax.fori_loop(early, PAIRS, add_far, 0)
    grad_normed = grad_normed + project_back(slice(early * LANES, D))
    normalized, inverse = normalize(hidden)
    scaled = grad_normed * gain
    inner = (
        scaled
        - jnp.mean(scaled, axis=1, keepdims=True)
        - normalized * jnp.mean(scaled * normalized, axis=1, keepdims=True)
    )
    grad_hidden = (og_ref[...].astype(F32) + inner * inverse).astype(BF16)

    rows_ref[...] = mm(unplace, grad_hidden)

    def pack_back(first, last):
        def step(i, carry):
            mine = rows_ref[pl.ds(pl.multiple_of(i * 8, 8), 8), :].astype(BF16)
            theirs = rows_ref[pl.ds(pl.multiple_of(PACKED // 2 + i * 8, 8), 8), :].astype(BF16)
            out2_ref[2 * i, core] = mine[0:4]
            out2_ref[2 * i + 1, core] = mine[4:8]
            out2_ref[2 * i, other_core] = theirs[0:4]
            out2_ref[2 * i + 1, other_core] = theirs[4:8]
            return carry

        lax.fori_loop(first // 2, last // 2, step, 0, unroll=8)

    exchange_start(1, out2_ref, mid2_ref, pack_back)

    layer_ref[...] = (hidden + mm(att_ref[...], wo_ref[...])).astype(BF16)
    exchange_sent(0, out_ref, mid_ref, over_ref)

    def sent(c):
        fifteen = far_ref.at[c, 0, pl.ds(0, HALF - FAR)]
        pltpu.make_async_copy(fifteen, fifteen, g_send.at[c]).wait()
        forward_copy(c).wait_send()
        half_copy(c).wait_send()
        parts = part_send.at[c, pl.ds(0, HALF - FAR)]
        pltpu.make_async_copy(parts, parts, p_send.at[c]).wait()

    loop(0, PAIRS, sent)

    exchange_arrive(1, out2_ref, mid2_ref, over2_ref)
    back = mm(pick_back[:, : PACKED // 2], rows_ref[: PACKED // 2].astype(BF16))
    over_rows(1, mid2_ref, over2_ref)
    back = back + mm(pick_back[:, PACKED // 2 :], rows_ref[PACKED // 2 :].astype(BF16))
    back_ref[...] = back.astype(BF16)
    exchange_sent(1, out2_ref, mid2_ref, over2_ref)


def per_device(tiles, dest_row, w_in, norm_gain, w_query, w_key, w_value, w_out, out_grad):
    vmem = pl.BlockSpec(memory_space=pltpu.VMEM)
    hbm = pl.BlockSpec(memory_space=pl.ANY)
    dma = pltpu.SemaphoreType.DMA
    slots = (ALL_CHIPS, 2, SLOTS, D)
    over = (ALL_CHIPS, SLOTS, D)
    pairs = (PAIRS, HALF, 2 * LANES)

    def bf16(*shape):
        return pltpu.VMEM(shape, BF16)

    def f32(*shape):
        return pltpu.VMEM(shape, F32)

    layer, grad_hidden = pl.pallas_call(
        block_kernel,
        out_shape=(jax.ShapeDtypeStruct((ROWS, D), BF16), jax.ShapeDtypeStruct((ROWS, D), BF16)),
        in_specs=[hbm, vmem, vmem] + [hbm] * 6,
        out_specs=(vmem, vmem),
        scratch_shapes=[
            bf16(ROWS, WIDTH), bf16(WIDTH, D), bf16(D, D), bf16(D, D), bf16(D, D), bf16(D, D), bf16(ROWS, D),
            f32(PACKED, D), bf16(*slots), bf16(*slots), bf16(*over), bf16(*slots), bf16(*slots), bf16(*over),
            bf16(ROWS, D), bf16(ROWS, D), bf16(ROWS, D), bf16(ROWS, D), bf16(ROWS, D),
            bf16(PAIRS, 2, HALF, 2 * LANES),
            bf16(ROWS, D), bf16(ROWS, D), f32(ROWS, D), f32(ROWS, D),
            bf16(PAIRS, 4 * ROWS, LANES), f32(PAIRS, ROWS, 4 * ROWS), f32(PAIRS, 8, 2 * ROWS),
            f32(2 * HALF, 4 * ROWS), bf16(PAIRS, ROWS + 2 * HALF, 4 * ROWS),
            f32(*pairs), bf16(*pairs), bf16(*pairs), bf16(*pairs), bf16(*pairs),
            dma((7,)), dma((2,)), dma((2, GROUPS)), dma((2, GROUPS)), dma((2, GROUPS)),
            dma((PAIRS,)), dma((PAIRS,)), dma((PAIRS,)), dma((PAIRS,)),
            dma((PAIRS,)), dma((PAIRS,)), dma((PAIRS,)), dma((PAIRS,)),
        ],
        compiler_params=pltpu.CompilerParams(
            vmem_limit_bytes=VMEM_LIMIT, collective_id=0, has_side_effects=True
        ),
    )(tiles, dest_row.reshape(ROWS, DEVICES), norm_gain, w_in, w_query, w_key, w_value, w_out, out_grad)
    return layer, mm_nt(grad_hidden, w_in).astype(BF16)


def solution(mesh):
    split = P(("slide", "seq"), None)
    return jax.shard_map(
        per_device,
        mesh=mesh,
        in_specs=(split, P(), P(), P(), P(), P(), P(), P(), split),
        out_specs=(split, split),
        check_vma=False,
    )
```
